128 devices in a mesh: ccd: 16 (over y, x_hi, core), amp: 8 (over x_lo, z).
Axes of the slice: x: 4 (x_hi: 2, x_lo: 2; x = x_hi * 2 + x_lo), y: 4, z: 4, core: 2. Of those that a mesh axis runs over, the one named last changes fastest.
Arguments:
- science: float32 [16, 1024, 4096], P('ccd', 'amp'), may hold values from -6 to 6
- patches: float32 [16, 8, 4, 256, 256], P('ccd', 'amp'), may hold values from -6 to 6
- coeffs: float32 [16, 40, 6], P('ccd'), may hold values from -0.9 to 0.9
- tile_owner: int32 [16, 8, 32, 1], replicated, may hold values from 0 to 15; in each aligned block of 32 rows (0 to 31, 32 to 63, ..., all dimensions but the last counted through in order) at most 4 rows name the same one
- tile_patch: int32 [16, 8, 32], replicated, may hold values from 0 to 3
- tile_offset: int32 [16, 8, 32, 2], replicated, may hold values from 0 to 128
Outputs:
- difference: float32 [16, 1024, 4096], P('ccd', 'amp')
The draws below stay inside these ranges and needn't reach their ends.
Inputs may be any that keep to these rules, and one draw needn't show every extreme that they name: `tile_owner`: among the 32 tiles of one strip, at most 4 name the same owner.
All inputs are finite; a program needn't handle non-finite values.
Results may differ from the reference program's by a relative error of at most 0.0031.
Values may be sent and summed in bfloat16 or wider, within the bound.
No kernel may reach another device: no remote copies, remote signals or barrier semaphores. Data moves between devices by JAX's collectives and lax.ppermute only.
A program may use at most 128 MiB of HBM per device.

```python
import math
import jax
import jax.numpy as jnp
import numpy as np
from jax import lax

W = 4096
TS = 128
PS = 256
PATCH_DEV = 4
HALF = 10
K = 40
NPOLY = 6
TROWS = 1
ROWS_DEV = 128
TILES_DEV = 32
CAP = 4
NROWS = 1024
N_CCD = 16
N_AMP = 8


def draw_patches(key, part):
    key = jax.random.fold_in(key, 11)
    patch_shape = (N_CCD, N_AMP, PATCH_DEV, PS, PS)
    return jnp.clip(jax.random.normal(key, patch_shape, jnp.float32), -6.0, 6.0)


def draw_coeffs(key, part):
    key = jax.random.fold_in(key, 23)
    coeff_shape = (N_CCD, K, NPOLY)
    return jnp.clip(0.15 * jax.random.normal(key, coeff_shape, jnp.float32), -0.9, 0.9)


def touch_ends(values, key, low, top_value):
    longest = values.shape.index(max(values.shape))
    spots = []
    for shift in (0, 1):
        where = [jax.random.randint(jax.random.fold_in(key, axis), (), 0, length) for axis, length in enumerate(values.shape)]
        where[longest] = (where[longest] + shift) % values.shape[longest]
        spots.append(tuple(where))
    return values.at[spots[0]].set(low).at[spots[1]].set(top_value)


def level_of(own_key, dims, shards, low, high):
    def one(position, blocks):
        heights = jax.random.uniform(jax.random.fold_in(jax.random.fold_in(own_key, 6), position), (blocks,), jnp.float32, low / len(shards), high / len(shards))
        return jnp.repeat(jnp.exp(heights), dims[position] // blocks).reshape((-1,) + (1,) * (len(dims) - position - 1))

    level = one(*shards[0])
    for cut in shards[1:]:
        level = level * one(*cut)
    return level


def routed_block(own_key, own, number, rows, number_of, top, most, slope):
    sequence = jax.random.permutation(own_key, number_of)
    packed, ordinary = portions_of(number_of, rows * top, most, slope, True), portions_of(number_of, rows * top, most, slope, False)
    places = jnp.arange(number_of)

    def named(tallies, offset_by):
        used = int((tallies > 0).sum())
        fixed = max(1, used // 4)
        passed = fixed + (places - fixed + offset_by * (used - fixed)) % max(1, number_of - fixed)
        return jnp.zeros((number_of,), jnp.int32).at[sequence[jnp.where(places < fixed, places, passed)]].set(jnp.asarray(tallies, jnp.int32))

    tallies = jnp.where(number % 4 == 0, named(packed, number // 4), named(ordinary, number - number // 4 - 1))
    mixed = jax.random.permutation(jax.random.fold_in(own, 3), number_of)
    donor, receiver = mixed[0:number_of // 2 * 2:2], mixed[1:number_of // 2 * 2:2]
    room = jnp.minimum(tallies[donor] - 1, most - tallies[receiver]) // 2
    room = jnp.where((donor == sequence[0]) | (receiver == sequence[0]) | (tallies[receiver] == 0), 0, jnp.maximum(room, 0))
    passed = jax.random.randint(jax.random.fold_in(own, 4), (number_of // 2,), 0, 1 << 20) % (room + 1)
    tallies = tallies.at[donor].add(-passed).at[receiver].add(passed)
    items = jnp.searchsorted(jnp.cumsum(tallies), jnp.arange(rows * top), side="right").astype(jnp.int32)
    grid = items.reshape(top, rows).T
    grid = grid[jax.random.permutation(jax.random.fold_in(own, 1), rows)]
    offset_by = jax.random.randint(jax.random.fold_in(own, 2), (rows, 1), 0, top)
    return jnp.take_along_axis(grid, (jnp.arange(top)[None, :] + offset_by) % top, axis=1)


def portions_of(count, total, bound, skew, full):
    loads = [(1 << 20) // math.isqrt(grade ** skew) + 1 for grade in range(1, count + 1)]
    largest = bound if full else min(bound, max(-(-total // count), total * loads[0] // sum(loads)))
    least = 1 if total - largest >= count - 1 else 0
    holding, rest = [largest] + [least] * (count - 1), total - largest - least * (count - 1)
    while rest > 0:
        free = [i for i in range(1, count) if holding[i] < largest] or [i for i in range(1, count) if holding[i] < bound]
        pool, left = sum([loads[i] for i in free]), rest
        for i in free:
            extra = min(bound - holding[i], max(1, left * loads[i] // pool), rest)
            holding[i] = holding[i] + extra
            rest = rest - extra
    return np.array(holding)


def centred(rng, shape, width, reach, cuts=(), kind=jnp.bfloat16):
    result = width * jax.random.normal(rng, shape, jnp.float32)
    if cuts:
        result = result * level_of(rng, shape, cuts, -0.22, 0.18)
    return jnp.clip(result, -reach, reach).astype(kind)


def setup_inputs(seed: int = 0) -> dict:
    key_of = jax.random.split(jax.random.key(seed), 7)
    science = centred(key_of[0], (N_CCD, NROWS, W), 1.0, 6.0, ((0, 16), (1, 8)), jnp.float32)
    patches = draw_patches(jax.random.fold_in(key_of[6], 71), 0)
    coeffs = draw_coeffs(jax.random.fold_in(key_of[6], 71), 0)
    tile_owner_keys = jax.random.split(jax.random.fold_in(key_of[3], 1), N_CCD * N_AMP * TILES_DEV // TILES_DEV)
    tile_owner_turns = jax.random.permutation(jax.random.fold_in(key_of[3], 3), N_CCD * N_AMP * TILES_DEV // TILES_DEV)
    tile_owner = jax.vmap(lambda own, number: routed_block(jax.random.fold_in(key_of[3], 2), own, number, TILES_DEV, N_CCD, 1, CAP, 2))(tile_owner_keys, tile_owner_turns).reshape((N_CCD, N_AMP, TILES_DEV, 1))
    tile_patch = touch_ends(jax.random.randint(key_of[4], (N_CCD, N_AMP, TILES_DEV), 0, PATCH_DEV), jax.random.fold_in(key_of[4], 1), 0, PATCH_DEV - 1).astype(jnp.int32)
    tile_offset = touch_ends(jax.random.randint(key_of[5], (N_CCD, N_AMP, TILES_DEV, 2), 0, PS - TS + 1), jax.random.fold_in(key_of[5], 1), 0, PS - TS).astype(jnp.int32)
    return {"science": science, "patches": patches, "coeffs": coeffs, "tile_owner": tile_owner, "tile_patch": tile_patch, "tile_offset": tile_offset}


gauss_widths = (1.0, 2.0, 4.0)
poly_degrees = (4, 4, 3)


def factor_table(half):
    offsets = jnp.arange(-half, half + 1).astype(jnp.float32)
    shapes = []
    for sigma_px, degree in zip(gauss_widths, poly_degrees):
        for exponent in range(degree + 1):
            profile = jnp.exp(-offsets * offsets / (2.0 * sigma_px * sigma_px)) * (offsets / half) ** exponent
            shapes.append(profile / jnp.sum(jnp.abs(profile)))
    return jnp.stack(shapes).astype(jnp.bfloat16)


def basis_groups():
    grouped_pairs = []
    first_factor = 0
    for degree in poly_degrees:
        members = []
        for across_pow in range(degree + 1):
            for down_pow in range(degree + 1 - across_pow):
                members.append((first_factor + across_pow, first_factor + down_pow))
        grouped_pairs.append(members)
        first_factor = first_factor + degree + 1
    return grouped_pairs


def across_matrices(factors, half):
    column = jnp.arange(256)[:, None]
    output = jnp.arange(128)[None, :]
    lag_cols = column - 64 - output
    tap_offsets = jnp.arange(-half, half + 1)
    select = (lag_cols[:, :, None] == tap_offsets[None, None, :]).astype(jnp.float32)
    mats = jnp.einsum('cqt,ht->hcq', select, factors.astype(jnp.float32), precision=lax.Precision.HIGHEST)
    return mats.astype(jnp.bfloat16)


def down_matrices(factors, half, strip_rows):
    target = jnp.arange(strip_rows)[:, None]
    source = jnp.arange(strip_rows + 2 * half)[None, :]
    lag_rows = source - half - target
    tap_offsets = jnp.arange(-half, half + 1)
    select = (lag_rows[:, :, None] == tap_offsets[None, None, :]).astype(jnp.float32)
    mats = jnp.einsum('yrt,ht->hyr', select, factors.astype(jnp.float32), precision=lax.Precision.HIGHEST)
    return mats.astype(jnp.bfloat16)


def strip_model(padded, coeff_rows, row_first, total_rows, across_mats, down_mats):
    padded_rows, columns = padded.shape
    strip_rows = padded_rows - 2 * HALF
    block_count = columns // 128
    blocks = padded.reshape(padded_rows, block_count, 128)
    empty_rim = jnp.zeros((padded_rows, 1, 64), padded.dtype)
    left_rim = jnp.concatenate([empty_rim, blocks[:, :-1, 64:]], axis=1)
    right_rim = jnp.concatenate([blocks[:, 1:, :64], empty_rim], axis=1)
    window = jnp.concatenate([left_rim, blocks, right_rim], axis=2)
    per_group = math.gcd(block_count, 8)
    group_count = block_count // per_group
    grouped = window.reshape(padded_rows, group_count, per_group, 256).transpose(1, 0, 2, 3)
    ycoord = (2.0 * (row_first + jnp.arange(strip_rows)).astype(jnp.float32) + 1.0) / total_rows - 1.0
    group_cols = per_group * 128

    def one_group(group_inputs):
        group_window, group_index = group_inputs
        xcoord = (2.0 * (group_index * group_cols + jnp.arange(group_cols)).astype(jnp.float32) + 1.0) / columns - 1.0
        xgrid = jnp.broadcast_to(xcoord[None, :], (strip_rows, group_cols))
        ygrid = jnp.broadcast_to(ycoord[:, None], (strip_rows, group_cols))
        poly_terms = jnp.stack([jnp.ones_like(xgrid), xgrid, ygrid, xgrid * xgrid, xgrid * ygrid, ygrid * ygrid])
        across_all = jnp.einsum('rbc,hcq->hrbq', group_window.astype(jnp.float32), across_mats.astype(jnp.float32), precision=lax.Precision.HIGHEST)
        across_all = across_all.astype(jnp.bfloat16).reshape(across_mats.shape[0], padded_rows, group_cols)
        psf_part = jnp.zeros((strip_rows, group_cols), jnp.float32)
        basis_first = 0
        for members in basis_groups():
            across_index = np.array([member[0] for member in members], dtype=np.int32)
            down_index = np.array([member[1] for member in members], dtype=np.int32)
            inputs = across_all[across_index].astype(jnp.float32)
            kernels = down_mats[down_index].astype(jnp.float32)
            convolved = jnp.einsum('kyr,krx->kyx', kernels, inputs, precision=lax.Precision.HIGHEST)
            weights = coeff_rows[basis_first:basis_first + len(members)]
            folded = jnp.einsum('km,kyx->myx', weights, convolved, precision=lax.Precision.HIGHEST)
            psf_part = psf_part + jnp.sum(folded * poly_terms, axis=0)
            basis_first = basis_first + len(members)
        return psf_part

    parts = lax.map(one_group, (grouped, jnp.arange(group_count, dtype=jnp.int32)))
    return parts.transpose(1, 0, 2).reshape(strip_rows, columns)


def assemble(patches, tile_owner, tile_patch, tile_offset):
    store_bf = patches.astype(jnp.bfloat16)
    amp_ids = jnp.broadcast_to(jnp.arange(N_AMP, dtype=jnp.int32)[None, :, None], (N_CCD, N_AMP, TILES_DEV))

    def crop(owner_id, amp_id, patch_id, row_shift, col_shift):
        start = (owner_id.astype(jnp.int32), amp_id.astype(jnp.int32), patch_id.astype(jnp.int32), row_shift.astype(jnp.int32), col_shift.astype(jnp.int32))
        return lax.dynamic_slice(store_bf, start, (1, 1, 1, TS, TS))[0, 0, 0]

    tile_stack = jax.vmap(crop)(tile_owner[..., 0].reshape(-1), amp_ids.reshape(-1), tile_patch.reshape(-1), tile_offset[..., 0].reshape(-1), tile_offset[..., 1].reshape(-1))
    tile_stack = tile_stack.reshape(N_CCD, N_AMP, TROWS, W // TS, TS, TS).transpose(0, 1, 2, 4, 3, 5)
    return tile_stack.reshape(N_CCD, NROWS, W)


def reference(science, patches, coeffs, tile_owner, tile_patch, tile_offset):
    template = assemble(patches, tile_owner, tile_patch, tile_offset)
    padded = jnp.pad(template, ((0, 0), (HALF, HALF), (0, 0)))
    factors = factor_table(HALF)
    across_mats = across_matrices(factors, HALF)
    down_mats = down_matrices(factors, HALF, ROWS_DEV)

    def one_ccd(ccd_inputs):
        padded_ccd, science_ccd, coeff_ccd = ccd_inputs

        def one_amp(amp_id):
            row_first = amp_id * ROWS_DEV
            strip_padded = lax.dynamic_slice_in_dim(padded_ccd, row_first, ROWS_DEV + 2 * HALF, 0)
            strip_science = lax.dynamic_slice_in_dim(science_ccd, row_first, ROWS_DEV, 0)
            return strip_science - strip_model(strip_padded, coeff_ccd, row_first, NROWS, across_mats, down_mats)

        strips = lax.map(one_amp, jnp.arange(N_AMP, dtype=jnp.int32))
        return strips.reshape(NROWS, W)

    return lax.map(one_ccd, (padded, science, coeffs))
```

```python
import numpy as np

import jax
import jax.numpy as jnp
import ml_dtypes
from jax import lax
from jax.experimental import pallas as pl
from jax.experimental.pallas import tpu as pltpu
from jax.sharding import PartitionSpec as P

TS = 128
HALF = 10
TAPS = 2 * HALF + 1
CAP = 4
WIDTHS = (1.0, 2.0, 4.0)
DEGREES = (4, 4, 3)
ROWS = 128
SIDE = 64
WIN = 80
EDGE = 16
K_MAIN = TAPS * WIN
K_PAD = 1792
K_EDGE = TAPS * EDGE
K_EDGE_PAD = 384
BLOCK = 256
MIB = 1 << 20


def factor_table():
    offsets = np.arange(-HALF, HALF + 1).astype(np.float64)
    shapes = []
    for width, degree in zip(WIDTHS, DEGREES):
        for power in range(degree + 1):
            profile = np.exp(-offsets * offsets / (2.0 * width * width)) * (offsets / HALF) ** power
            shapes.append(profile / np.sum(np.abs(profile)))
    return np.stack(shapes).astype(np.float32).astype(ml_dtypes.bfloat16).astype(np.float32)


def basis_table():
    factors = factor_table()
    rows = []
    first = 0
    for degree in DEGREES:
        for p in range(degree + 1):
            for q in range(degree + 1 - p):
                grid = np.zeros((TAPS, 128), np.float32)
                grid[:, :TAPS] = factors[first + p][:, None] * factors[first + q][None, :]
                rows.append(grid.reshape(-1))
        first += degree + 1
    return np.stack(rows)


def cut_kernel(table, patches, send):
    me = table[16, 0]

    def strip(d, carry):
        def tile(q, count):
            code = table[d, q]
            mine = (code & 15) == me

            @pl.when(mine)
            def _():
                patch = (code >> 4) & 3
                dy = (code >> 6) & 255
                dx = (code >> 14) & 255
                first = pl.multiple_of(lax.min((dy >> 3) << 3, 120), 8)
                rows = patches[patch, pl.ds(first, TS + 8), :]
                turned = pltpu.roll(rows, lax.rem(256 - dx, 256), 1)[:, :TS]
                turned = pltpu.roll(turned, lax.rem(TS + 8 - (dy - first), TS + 8), 0)
                send[d * CAP + count] = turned[:TS].astype(jnp.bfloat16)

            return count + mine.astype(jnp.int32)

        lax.fori_loop(0, 32, tile, jnp.int32(0), unroll=8)
        return carry

    lax.fori_loop(0, 16, strip, 0)


def weights_kernel(amp, moments, main, edge):
    first_row = amp[0] * ROWS
    lane = lax.broadcasted_iota(jnp.int32, (SIDE, 128), 1)
    lane16 = lax.broadcasted_iota(jnp.int32, (EDGE, 128), 1)

    def across(rows, members, yh):
        total = jnp.broadcast_to(rows[members[0] : members[0] + 1], (yh.shape[0], 128))
        for power, member in enumerate(members[1:]):
            total = total + (yh if power == 0 else yh * yh) * rows[member : member + 1]
        return pltpu.roll(total, 0, 1, stride=1, stride_axis=0)

    for half in range(2):
        y = (first_row + half * SIDE + lax.broadcasted_iota(jnp.int32, (SIDE, 128), 0)).astype(jnp.float32)
        yh = (2.0 * y + 1.0) / 1024.0 - 1.0
        rim = slice(0, EDGE) if half == 0 else slice(SIDE - EDGE, SIDE)
        lead = 6 if half else -HALF
        rim_lead = EDGE - HALF if half == 0 else SIDE - EDGE + 6 - WIN
        for a, members in enumerate(((0, 2, 5), (1, 4), (3,))):
            held = jnp.zeros((SIDE, 128), jnp.float32)
            held_rim = jnp.zeros((EDGE, 128), jnp.float32)
            for u in range(TAPS):
                moment = moments[:, u * 128 : (u + 1) * 128]
                last = u == TAPS - 1
                group, low = u * WIN // 128, u * WIN % 128
                end = low + WIN
                turned = across(pltpu.roll(moment, (lead + low) % 128, 1), members, yh)
                held = jnp.where((lane >= low) & (lane < end), turned, held)
                at = slice(a * SIDE, (a + 1) * SIDE)
                if end >= 128 or last:
                    main[half, at, group * 128 : (group + 1) * 128] = held.astype(jnp.bfloat16)
                    held = jnp.where(lane < end - 128, turned, 0.0)
                    if last and end > 128:
                        main[half, at, (group + 1) * 128 : (group + 2) * 128] = held.astype(jnp.bfloat16)
                group, low = u * EDGE // 128, u * EDGE % 128
                turned = across(pltpu.roll(moment, (rim_lead + low) % 128, 1), members, yh[rim])
                held_rim = jnp.where((lane16 >= low) & (lane16 < low + EDGE), turned, held_rim)
                if low + EDGE == 128 or last:
                    at = slice(a * EDGE, (a + 1) * EDGE)
                    edge[half, at, group * 128 : (group + 1) * 128] = held_rim.astype(jnp.bfloat16)
                    held_rim = jnp.zeros((EDGE, 128), jnp.float32)


def edge_kernel(slots, tiles, top, bottom):
    for q in range(32):
        at = slice(q * TS, (q + 1) * TS)
        top[:, at] = tiles[slots[q], 0:EDGE, :]
        bottom[:, at] = tiles[slots[q], TS - EDGE : TS, :]


def x_of(block, rows):
    x = block * BLOCK + lax.broadcasted_iota(jnp.int32, (rows, BLOCK), 1)
    return (2.0 * x.astype(jnp.float32) + 1.0) / 4096.0 - 1.0


def fold(parts, xh, rows):
    return parts[:rows] + xh * (parts[rows : 2 * rows] + xh * parts[2 * rows :])


def main_kernel(slots, tiles, weights, science, out, shifted):
    block = pl.program_id(0)
    left = tiles[slots[lax.max(2 * block - 1, 0)]]
    right = tiles[slots[lax.min(2 * block + 2, 31)]]
    left = jnp.where(block > 0, left, jnp.zeros_like(left))
    right = jnp.where(block < 15, right, jnp.zeros_like(right))
    window = jnp.concatenate([left, tiles[slots[2 * block]], tiles[slots[2 * block + 1]], right], axis=1)
    for u in range(TAPS):
        shifted[u] = window[:, 128 + u - HALF : 128 + u - HALF + BLOCK]
    xh = x_of(block, SIDE)
    for half in range(2):
        source = shifted[:, half * 48 : half * 48 + WIN, :].reshape(K_MAIN, BLOCK)
        parts = jnp.dot(weights[half, :, :K_MAIN], source, preferred_element_type=jnp.float32)
        at = slice(half * SIDE, (half + 1) * SIDE)
        out[at, :] = science[at, :] - fold(parts, xh, SIDE)


def rim_kernel(rows, before, here, after, weights, partial, out):
    half, block = pl.program_id(0), pl.program_id(1)
    keep = rows[half]
    left, right = before[0, :, 128:], after[0, :, :128]
    left = jnp.where(block > 0, left, jnp.zeros_like(left))
    right = jnp.where(block < 15, right, jnp.zeros_like(right))
    window = jnp.concatenate([left, here[0], right], axis=1)
    window = jnp.where(keep > 0, window, jnp.zeros_like(window))
    source = jnp.concatenate([window[:, 128 + u - HALF : 128 + u - HALF + BLOCK] for u in range(TAPS)], axis=0)
    parts = jnp.dot(weights[0, :, :K_EDGE], source, preferred_element_type=jnp.float32)
    out[...] = partial[...] - fold(parts, x_of(block, EDGE), EDGE)


def per_device(science, patches, coeffs, tile_owner, tile_patch, tile_offset):
    ccd_id = lax.axis_index("ccd")
    amp_id = lax.axis_index("amp")
    take = lambda array: lax.dynamic_index_in_dim(array, amp_id, 1, keepdims=False)
    shift = take(tile_offset)
    code = take(tile_owner)[..., 0] | (take(tile_patch) << 4) | (shift[..., 0] << 6) | (shift[..., 1] << 14)
    table = jnp.concatenate([code, jnp.full((1, 32), ccd_id, jnp.int32)], axis=0)

    whole = pl.BlockSpec(memory_space=pltpu.VMEM)
    scalars = pl.BlockSpec(memory_space=pltpu.SMEM)
    send = pl.pallas_call(
        cut_kernel,
        out_shape=jax.ShapeDtypeStruct((16 * CAP, TS, TS), jnp.bfloat16),
        in_specs=[scalars, whole],
        out_specs=whole,
        compiler_params=pltpu.CompilerParams(vmem_limit_bytes=24 * MIB),
        name="cut",
    )(table, patches.reshape(4, 256, 256))
    tiles = lax.all_to_all(send.reshape(16, CAP * TS, TS), "ccd", 0, 0, tiled=True).reshape(16 * CAP, TS, TS)

    mine = lax.dynamic_index_in_dim(code, ccd_id, 0, keepdims=False) & 15
    earlier = (mine[:, None] == mine[None, :]) & (jnp.arange(32)[None, :] < jnp.arange(32)[:, None])
    slots = mine * CAP + jnp.minimum(jnp.sum(earlier.astype(jnp.int32), axis=1), CAP - 1)

    moments = jnp.einsum("km,kl->ml", coeffs[0], jnp.asarray(basis_table()), precision=lax.Precision.HIGHEST)
    main, edge = pl.pallas_call(
        weights_kernel,
        out_shape=(
            jax.ShapeDtypeStruct((2, 3 * SIDE, K_PAD), jnp.bfloat16),
            jax.ShapeDtypeStruct((2, 3 * EDGE, K_EDGE_PAD), jnp.bfloat16),
        ),
        in_specs=[scalars, whole],
        out_specs=(whole, whole),
        compiler_params=pltpu.CompilerParams(vmem_limit_bytes=24 * MIB),
        cost_estimate=pl.CostEstimate(flops=50_000_000, bytes_accessed=2_000_000, transcendentals=0),
        name="weights",
    )(amp_id.reshape(1), moments)

    top, bottom = pl.pallas_call(
        edge_kernel,
        out_shape=(jax.ShapeDtypeStruct((EDGE, 4096), jnp.bfloat16),) * 2,
        in_specs=[scalars, whole],
        out_specs=(whole, whole),
        compiler_params=pltpu.CompilerParams(vmem_limit_bytes=24 * MIB),
        name="edges",
    )(slots, tiles)
    down = [(i, i + 1) for i in range(7)]
    above = lax.ppermute(bottom, "amp", down)
    below = lax.ppermute(top, "amp", [(b, a) for a, b in down])

    partial = pl.pallas_call(
        main_kernel,
        grid_spec=pltpu.PrefetchScalarGridSpec(
            num_scalar_prefetch=1,
            grid=(16,),
            in_specs=[
                whole,
                whole,
                pl.BlockSpec((ROWS, BLOCK), lambda j, s: (0, j)),
            ],
            out_specs=pl.BlockSpec((ROWS, BLOCK), lambda j, s: (0, j)),
            scratch_shapes=[pltpu.VMEM((TAPS, ROWS, BLOCK), jnp.bfloat16)],
        ),
        out_shape=jax.ShapeDtypeStruct((ROWS, 4096), jnp.float32),
        compiler_params=pltpu.CompilerParams(vmem_limit_bytes=32 * MIB),
        cost_estimate=pl.CostEstimate(flops=11_000_000_000, bytes_accessed=8_000_000, transcendentals=0),
        name="main",
    )(slots, tiles, main, science[0])

    rims = jnp.stack([above, below])
    inner = jnp.stack([amp_id > 0, amp_id < 7]).astype(jnp.int32)
    result = pl.pallas_call(
        rim_kernel,
        grid_spec=pltpu.PrefetchScalarGridSpec(
            num_scalar_prefetch=1,
            grid=(2, 16),
            in_specs=[
                pl.BlockSpec((1, EDGE, BLOCK), lambda h, j, s: (h, 0, jnp.maximum(j - 1, 0))),
                pl.BlockSpec((1, EDGE, BLOCK), lambda h, j, s: (h, 0, j)),
                pl.BlockSpec((1, EDGE, BLOCK), lambda h, j, s: (h, 0, jnp.minimum(j + 1, 15))),
                pl.BlockSpec((1, 3 * EDGE, K_EDGE_PAD), lambda h, j, s: (h, 0, 0)),
                pl.BlockSpec((EDGE, BLOCK), lambda h, j, s: (7 * h, j)),
            ],
            out_specs=pl.BlockSpec((EDGE, BLOCK), lambda h, j, s: (7 * h, j)),
        ),
        out_shape=jax.ShapeDtypeStruct((ROWS, 4096), jnp.float32),
        input_output_aliases={5: 0},
        compiler_params=pltpu.CompilerParams(vmem_limit_bytes=24 * MIB),
        name="rim",
    )(inner, rims, rims, rims, edge, partial)
    return result[None]


def solution(mesh):
    placed = (
        P("ccd", "amp", None),
        P("ccd", "amp", None, None, None),
        P("ccd", None, None),
        P(),
        P(),
        P(),
    )
    return jax.shard_map(
        per_device, mesh=mesh, in_specs=placed, out_specs=P("ccd", "amp", None), check_vma=False
    )
```

```python
import numpy as np

import jax
import jax.numpy as jnp
import ml_dtypes
from jax import lax
from jax.experimental import pallas as pl
from jax.experimental.pallas import tpu as pltpu
from jax.sharding import PartitionSpec as P

TS = 128
HALF = 10
TAPS = 2 * HALF + 1
CAP = 4
WIDTHS = (1.0, 2.0, 4.0)
DEGREES = (4, 4, 3)
ROWS = 128
SIDE = 64
WIN = 80
EDGE = 16
K_MAIN = TAPS * WIN
K_PAD = 1792
K_EDGE = TAPS * EDGE
K_EDGE_PAD = 384
BLOCK = 512
TILES = BLOCK // TS
CUT = 16
MIB = 1 << 20


def factor_table():
    offsets = np.arange(-HALF, HALF + 1).astype(np.float64)
    shapes = []
    for width, degree in zip(WIDTHS, DEGREES):
        for power in range(degree + 1):
            profile = np.exp(-offsets * offsets / (2.0 * width * width)) * (offsets / HALF) ** power
            shapes.append(profile / np.sum(np.abs(profile)))
    return np.stack(shapes).astype(np.float32).astype(ml_dtypes.bfloat16).astype(np.float32)


def basis_table():
    factors = factor_table()
    rows = []
    first = 0
    for degree in DEGREES:
        for p in range(degree + 1):
            for q in range(degree + 1 - p):
                grid = np.zeros((TAPS, 128), np.float32)
                grid[:, :TAPS] = factors[first + p][:, None] * factors[first + q][None, :]
                rows.append(grid.reshape(-1))
        first += degree + 1
    return np.stack(rows)


def cut_kernel(table, patches, send, halves):
    step = pl.program_id(0)

    @pl.when(step == 0)
    def _():
        for patch in range(4):
            for side in range(2):
                at = (patch * 2 + side) * 256
                halves[at : at + 256, :] = patches[patch, :, side * TS : (side + 1) * TS]

    lane = lax.broadcasted_iota(jnp.int32, (TS, TS), 1)

    def tile(slot, carry):
        code = table[step * CUT + slot]
        at = ((code >> 4) & 3) * 512 + ((code >> 6) & 255)
        dx = (code >> 14) & 255
        turn = (TS - dx) & (TS - 1)
        low = pltpu.roll(halves[pl.ds(at, TS), :], turn, 1)
        high = pltpu.roll(halves[pl.ds(at + 256, TS), :], turn, 1)
        send[slot] = jnp.where(lane < TS - dx, low, high).astype(jnp.bfloat16)
        return carry

    lax.fori_loop(0, CUT, tile, 0, unroll=4)


def weights_kernel(amp, moments, main, edge):
    first_row = amp[0] * ROWS
    lane = lax.broadcasted_iota(jnp.int32, (SIDE, 128), 1)
    lane16 = lax.broadcasted_iota(jnp.int32, (EDGE, 128), 1)

    def across(rows, members, yh):
        total = jnp.broadcast_to(rows[members[0] : members[0] + 1], (yh.shape[0], 128))
        for power, member in enumerate(members[1:]):
            total = total + (yh if power == 0 else yh * yh) * rows[member : member + 1]
        return pltpu.roll(total, 0, 1, stride=1, stride_axis=0)

    for half in range(2):
        y = (first_row + half * SIDE + lax.broadcasted_iota(jnp.int32, (SIDE, 128), 0)).astype(jnp.float32)
        yh = (2.0 * y + 1.0) / 1024.0 - 1.0
        rim = slice(0, EDGE) if half == 0 else slice(SIDE - EDGE, SIDE)
        lead = 6 if half else -HALF
        rim_lead = EDGE - HALF if half == 0 else SIDE - EDGE + 6 - WIN
        for a, members in enumerate(((0, 2, 5), (1, 4), (3,))):
            held = jnp.zeros((SIDE, 128), jnp.float32)
            held_rim = jnp.zeros((EDGE, 128), jnp.float32)
            for u in range(TAPS):
                moment = moments[:, u * 128 : (u + 1) * 128]
                last = u == TAPS - 1
                group, low = u * WIN // 128, u * WIN % 128
                end = low + WIN
                turned = across(pltpu.roll(moment, (lead + low) % 128, 1), members, yh)
                held = jnp.where((lane >= low) & (lane < end), turned, held)
                at = slice(a * SIDE, (a + 1) * SIDE)
                if end >= 128 or last:
                    main[half, at, group * 128 : (group + 1) * 128] = held.astype(jnp.bfloat16)
                    held = jnp.where(lane < end - 128, turned, 0.0)
                    if last and end > 128:
                        main[half, at, (group + 1) * 128 : (group + 2) * 128] = held.astype(jnp.bfloat16)
                group, low = u * EDGE // 128, u * EDGE % 128
                turned = across(pltpu.roll(moment, (rim_lead + low) % 128, 1), members, yh[rim])
                held_rim = jnp.where((lane16 >= low) & (lane16 < low + EDGE), turned, held_rim)
                if low + EDGE == 128 or last:
                    at = slice(a * EDGE, (a + 1) * EDGE)
                    edge[half, at, group * 128 : (group + 1) * 128] = held_rim.astype(jnp.bfloat16)
                    held_rim = jnp.zeros((EDGE, 128), jnp.float32)


def edge_kernel(slots, tiles, top, bottom):
    for q in range(32):
        at = slice(q * TS, (q + 1) * TS)
        top[:, at] = tiles[slots[q], 0:EDGE, :]
        bottom[:, at] = tiles[slots[q], TS - EDGE : TS, :]


def x_of(first, shape):
    x = first + lax.broadcasted_iota(jnp.int32, shape, 1)
    return (2.0 * x.astype(jnp.float32) + 1.0) / 4096.0 - 1.0


def fold(parts, xh):
    rows = xh.shape[0]
    return parts[:rows] + xh * (parts[rows : 2 * rows] + xh * parts[2 * rows :])


def shifted_by(tiles, lag):
    if lag == 0:
        return tiles[1:-1]
    lane = lax.broadcasted_iota(jnp.int32, tiles[0].shape, 1)
    turned = [pltpu.roll(tile, (-lag) % TS, 1) for tile in tiles]
    if lag > 0:
        return [jnp.where(lane < TS - lag, turned[i], turned[i + 1]) for i in range(1, len(tiles) - 1)]
    return [jnp.where(lane < -lag, turned[i - 1], turned[i]) for i in range(1, len(tiles) - 1)]


def main_kernel(slots, tiles, weights, science, out, even, odd):
    step = pl.program_id(0)

    def shift(first, buffer):
        near = [tiles[slots[jnp.clip(first + i, 0, 31)]] for i in range(-1, TILES + 1)]
        near[0] = jnp.where(first > 0, near[0], jnp.zeros_like(near[0]))
        near[-1] = jnp.where(first + TILES < 32, near[-1], jnp.zeros_like(near[-1]))
        for u in range(TAPS):
            for i, tile in enumerate(shifted_by(near, u - HALF)):
                buffer[u, :, i * TS : (i + 1) * TS] = tile

    def multiply(first, buffer, columns):
        xh = x_of(first * TS, (SIDE, BLOCK))
        for half in range(2):
            source = buffer[:, half * 48 : half * 48 + WIN, :].reshape(K_MAIN, BLOCK)
            parts = jnp.dot(weights[half, :, :K_MAIN], source, preferred_element_type=jnp.float32)
            at = slice(half * SIDE, (half + 1) * SIDE)
            out[at, columns] = science[at, columns] - fold(parts, xh)

    @pl.when(step == 0)
    def _():
        shift(0, even)

    first = step * 2 * TILES
    shift(first + TILES, odd)
    multiply(first, even, slice(0, BLOCK))
    shift(first + 2 * TILES, even)
    multiply(first + TILES, odd, slice(BLOCK, 2 * BLOCK))


def rim_kernel(inner, above, below, weights, partial, out):
    step = pl.program_id(0)
    zero = jnp.zeros((EDGE, TS), jnp.bfloat16)

    def side(rows, number):
        keep = inner[number] > 0
        for first in range(0, 32, TILES):
            near = [
                rows[:, q * TS : (q + 1) * TS] if 0 <= q < 32 else zero for q in range(first - 1, first + TILES + 1)
            ]
            near = [jnp.where(keep, tile, zero) for tile in near]
            source = jnp.concatenate(
                [jnp.concatenate(shifted_by(near, u - HALF), axis=1) for u in range(TAPS)], axis=0
            )
            parts = jnp.dot(weights[number, :, :K_EDGE], source, preferred_element_type=jnp.float32)
            at = slice(first * TS, (first + TILES) * TS)
            out[:, at] = partial[:, at] - fold(parts, x_of(first * TS, (EDGE, BLOCK)))

    @pl.when(step == 0)
    def _():
        side(above, 0)

    @pl.when(step == 1)
    def _():
        side(below, 1)


def per_device(science, patches, coeffs, tile_owner, tile_patch, tile_offset):
    ccd_id = lax.axis_index("ccd")
    amp_id = lax.axis_index("amp")
    take = lambda array: lax.dynamic_index_in_dim(array, amp_id, 1, keepdims=False)
    shift = take(tile_offset)
    code = take(tile_owner)[..., 0] | (take(tile_patch) << 4) | (shift[..., 0] << 6) | (shift[..., 1] << 14)
    order = jnp.arange(32)
    named = code & 15
    chosen = named == ccd_id
    rank = jnp.sum((chosen[:, None, :] & (order[None, None, :] < order[None, :, None])).astype(jnp.int32), axis=2)
    place = chosen[:, None, :] & (rank[:, None, :] == jnp.arange(CAP)[None, :, None])
    table = jnp.sum(jnp.where(place, code[:, None, :], 0), axis=2).reshape(-1)

    whole = pl.BlockSpec(memory_space=pltpu.VMEM)
    scalars = pl.BlockSpec(memory_space=pltpu.SMEM)
    send = pl.pallas_call(
        cut_kernel,
        grid=(16 * CAP // CUT,),
        out_shape=jax.ShapeDtypeStruct((16 * CAP, TS, TS), jnp.bfloat16),
        in_specs=[scalars, whole],
        out_specs=pl.BlockSpec((CUT, TS, TS), lambda i: (i, 0, 0)),
        scratch_shapes=[pltpu.VMEM((4 * 2 * 256, TS), jnp.float32)],
        compiler_params=pltpu.CompilerParams(vmem_limit_bytes=24 * MIB),
        name="cut",
    )(table, patches.reshape(4, 256, 256))
    tiles = lax.all_to_all(send.reshape(16, CAP * TS, TS), "ccd", 0, 0, tiled=True).reshape(16 * CAP, TS, TS)

    mine = lax.dynamic_index_in_dim(named, ccd_id, 0, keepdims=False)
    earlier = (mine[:, None] == mine[None, :]) & (order[None, :] < order[:, None])
    slots = mine * CAP + jnp.minimum(jnp.sum(earlier.astype(jnp.int32), axis=1), CAP - 1)

    moments = jnp.einsum("km,kl->ml", coeffs[0], jnp.asarray(basis_table()), precision=lax.Precision.HIGHEST)
    main, edge = pl.pallas_call(
        weights_kernel,
        out_shape=(
            jax.ShapeDtypeStruct((2, 3 * SIDE, K_PAD), jnp.bfloat16),
            jax.ShapeDtypeStruct((2, 3 * EDGE, K_EDGE_PAD), jnp.bfloat16),
        ),
        in_specs=[scalars, whole],
        out_specs=(whole, whole),
        compiler_params=pltpu.CompilerParams(vmem_limit_bytes=24 * MIB),
        cost_estimate=pl.CostEstimate(flops=50_000_000, bytes_accessed=2_000_000, transcendentals=0),
        name="weights",
    )(amp_id.reshape(1), moments)

    top, bottom = pl.pallas_call(
        edge_kernel,
        out_shape=(jax.ShapeDtypeStruct((EDGE, 4096), jnp.bfloat16),) * 2,
        in_specs=[scalars, whole],
        out_specs=(whole, whole),
        compiler_params=pltpu.CompilerParams(vmem_limit_bytes=24 * MIB),
        name="edges",
    )(slots, tiles)
    down = [(i, i + 1) for i in range(7)]
    above = lax.ppermute(bottom, "amp", down)
    below = lax.ppermute(top, "amp", [(b, a) for a, b in down])

    columns = pl.BlockSpec((ROWS, 2 * BLOCK), lambda j, s: (0, j))
    partial = pl.pallas_call(
        main_kernel,
        grid_spec=pltpu.PrefetchScalarGridSpec(
            num_scalar_prefetch=1,
            grid=(4096 // (2 * BLOCK),),
            in_specs=[whole, whole, columns],
            out_specs=columns,
            scratch_shapes=[pltpu.VMEM((TAPS, ROWS, BLOCK), jnp.bfloat16)] * 2,
        ),
        out_shape=jax.ShapeDtypeStruct((ROWS, 4096), jnp.float32),
        compiler_params=pltpu.CompilerParams(vmem_limit_bytes=32 * MIB),
        cost_estimate=pl.CostEstimate(flops=11_000_000_000, bytes_accessed=8_000_000, transcendentals=0),
        name="main",
    )(slots, tiles, main, science[0])

    inner = jnp.stack([amp_id > 0, amp_id < 7]).astype(jnp.int32)
    strip_end = pl.BlockSpec((EDGE, 4096), lambda h, s: (7 * h, 0))
    result = pl.pallas_call(
        rim_kernel,
        grid_spec=pltpu.PrefetchScalarGridSpec(
            num_scalar_prefetch=1,
            grid=(2,),
            in_specs=[whole, whole, whole, strip_end],
            out_specs=strip_end,
        ),
        out_shape=jax.ShapeDtypeStruct((ROWS, 4096), jnp.float32),
        input_output_aliases={4: 0},
        compiler_params=pltpu.CompilerParams(vmem_limit_bytes=24 * MIB),
        name="rim",
    )(inner, above, below, edge, partial)
    return result[None]


def solution(mesh):
    placed = (
        P("ccd", "amp", None),
        P("ccd", "amp", None, None, None),
        P("ccd", None, None),
        P(),
        P(),
        P(),
    )
    return jax.shard_map(
        per_device, mesh=mesh, in_specs=placed, out_specs=P("ccd", "amp", None), check_vma=False
    )
```

```python
import numpy as np

import jax
import jax.numpy as jnp
import ml_dtypes
from jax import lax
from jax.experimental import pallas as pl
from jax.experimental.pallas import tpu as pltpu
from jax.sharding import PartitionSpec as P

TS = 128
HALF = 10
TAPS = 2 * HALF + 1
CAP = 4
WIDTHS = (1.0, 2.0, 4.0)
DEGREES = (4, 4, 3)
ROWS = 128
SIDE = 64
WIN = 80
EDGE = 16
K_MAIN = (TAPS + 1) * WIN
K_PAD = 1792
K_EDGE = (TAPS + 1) * EDGE
K_EDGE_PAD = 384
BLOCK = 512
WIDE = BLOCK // 2
TILES = WIDE // TS
LAGS = TAPS + 1
CUT = 16
MIB = 1 << 20


def factor_table():
    offsets = np.arange(-HALF, HALF + 1).astype(np.float64)
    shapes = []
    for width, degree in zip(WIDTHS, DEGREES):
        for power in range(degree + 1):
            profile = np.exp(-offsets * offsets / (2.0 * width * width)) * (offsets / HALF) ** power
            shapes.append(profile / np.sum(np.abs(profile)))
    return np.stack(shapes).astype(np.float32).astype(ml_dtypes.bfloat16).astype(np.float32)


def basis_table():
    factors = factor_table()
    rows = []
    first = 0
    for degree in DEGREES:
        for p in range(degree + 1):
            for q in range(degree + 1 - p):
                grid = np.zeros((TAPS, 128), np.float32)
                grid[:, :TAPS] = factors[first + p][:, None] * factors[first + q][None, :]
                rows.append(grid.reshape(-1))
        first += degree + 1
    return np.stack(rows)


def cut_kernel(here, codes, patches, send, halves, listed, table, sems, table_sem):
    step = pl.program_id(0)

    @pl.when(step == 0)
    def _():
        copies = [
            pltpu.make_async_copy(
                patches.at[patch, :, pl.ds(side * TS, TS)],
                halves.at[pl.ds((patch * 2 + side) * 256, 256), :],
                sems.at[patch, side],
            )
            for patch in range(4)
            for side in range(2)
        ]
        for copy in copies:
            copy.start()
        code = codes[here[0]]
        mine = (code & 15) == here[1]
        earlier = lax.broadcasted_iota(jnp.int32, (32, 32), 0) < lax.broadcasted_iota(jnp.int32, (32, 32), 1)
        as_bf16 = lambda mask: mask.astype(jnp.float32).astype(jnp.bfloat16)
        rank = jnp.dot(as_bf16(mine), as_bf16(earlier), preferred_element_type=jnp.float32)
        code = code.astype(jnp.float32)
        lane = lax.broadcasted_iota(jnp.int32, (16, 128), 1)
        total = jnp.zeros((16, 128), jnp.float32)
        for k in range(CAP):
            found = jnp.sum(jnp.where(mine & (rank == k), code, 0.0), axis=1, keepdims=True)
            total = jnp.where(lane == k, found, total)
        listed[...] = total.astype(jnp.int32)
        copy = pltpu.make_async_copy(listed, table, table_sem)
        copy.start()
        copy.wait()
        for copy in copies:
            copy.wait()

    lane = lax.broadcasted_iota(jnp.int32, (TS, TS), 1)

    def tile(slot, carry):
        code = table[step * (CUT // CAP) + slot // CAP, slot % CAP]
        at = ((code >> 4) & 3) * 512 + ((code >> 6) & 255)
        dx = (code >> 14) & 255
        turn = (TS - dx) & (TS - 1)
        low = pltpu.roll(halves[pl.ds(at, TS), :], turn, 1)
        high = pltpu.roll(halves[pl.ds(at + 256, TS), :], turn, 1)
        send[slot] = jnp.where(lane < TS - dx, low, high).astype(jnp.bfloat16)
        return carry

    lax.fori_loop(0, CUT, tile, 0, unroll=4)


def weights_kernel(amp, moments, main, edge):
    first_row = amp[0] * ROWS
    lane = lax.broadcasted_iota(jnp.int32, (SIDE, 128), 1)
    lane16 = lax.broadcasted_iota(jnp.int32, (EDGE, 128), 1)

    def across(rows, members, yh):
        total = jnp.broadcast_to(rows[members[0] : members[0] + 1], (yh.shape[0], 128))
        for power, member in enumerate(members[1:]):
            total = total + (yh if power == 0 else yh * yh) * rows[member : member + 1]
        return pltpu.roll(total, 0, 1, stride=1, stride_axis=0)

    for half in range(2):
        y = (first_row + half * SIDE + lax.broadcasted_iota(jnp.int32, (SIDE, 128), 0)).astype(jnp.float32)
        yh = (2.0 * y + 1.0) / 1024.0 - 1.0
        rim = slice(0, EDGE) if half == 0 else slice(SIDE - EDGE, SIDE)
        lead = 6 if half else -HALF
        rim_lead = EDGE - HALF if half == 0 else SIDE - EDGE + 6 - WIN
        for a, members in enumerate(((0, 2, 5), (1, 4), (3,))):
            held = jnp.zeros((SIDE, 128), jnp.float32)
            held_rim = jnp.zeros((EDGE, 128), jnp.float32)
            for u in range(TAPS):
                moment = moments[:, u * 128 : (u + 1) * 128]
                last = u == TAPS - 1
                group, low = u * WIN // 128, u * WIN % 128
                end = low + WIN
                turned = across(pltpu.roll(moment, (lead + low) % 128, 1), members, yh)
                held = jnp.where((lane >= low) & (lane < end), turned, held)
                at = slice(a * SIDE, (a + 1) * SIDE)
                if end >= 128 or last:
                    main[half, at, group * 128 : (group + 1) * 128] = held.astype(jnp.bfloat16)
                    held = jnp.where(lane < end - 128, turned, 0.0)
                    if last and end > 128:
                        main[half, at, (group + 1) * 128 : (group + 2) * 128] = held.astype(jnp.bfloat16)
                group, low = u * EDGE // 128, u * EDGE % 128
                turned = across(pltpu.roll(moment, (rim_lead + low) % 128, 1), members, yh[rim])
                held_rim = jnp.where((lane16 >= low) & (lane16 < low + EDGE), turned, held_rim)
                if low + EDGE == 128 or last:
                    at = slice(a * EDGE, (a + 1) * EDGE)
                    edge[half, at, group * 128 : (group + 1) * 128] = held_rim.astype(jnp.bfloat16)
                    held_rim = jnp.zeros((EDGE, 128), jnp.float32)
        main[half, 3 * SIDE :, :] = pltpu.roll(main[half, : 3 * SIDE, :], WIN, 1)
        edge[half, 3 * EDGE :, :] = pltpu.roll(edge[half, : 3 * EDGE, :], EDGE, 1)


def apart(transposed):
    wide, narrow = (1, 0) if transposed else (0, 1)
    column = lax.broadcasted_iota(jnp.int32, (256, 256), wide)
    place = lax.broadcasted_iota(jnp.int32, (256, 256), narrow)
    home = jnp.where(place < TS, 2 * place, 2 * place - 255)
    return (column == home).astype(jnp.float32).astype(jnp.bfloat16)


def phase_kernel(slots, tiles, planes, top, bottom):
    split = apart(False)
    for pair in range(16):
        both = jnp.concatenate([tiles[slots[2 * pair]], tiles[slots[2 * pair + 1]]], axis=1)
        moved = jnp.dot(both, split, preferred_element_type=jnp.float32).astype(jnp.bfloat16)
        for phase in range(2):
            piece = moved[:, phase * TS : (phase + 1) * TS]
            planes[phase, :, pair * TS : (pair + 1) * TS] = piece
            at = slice(phase * 2048 + pair * TS, phase * 2048 + (pair + 1) * TS)
            top[:, at] = piece[:EDGE]
            bottom[:, at] = piece[TS - EDGE :]


def fold(parts, first, rows):
    folded = []
    for phase in range(2):
        x = 2 * (first + lax.broadcasted_iota(jnp.int32, (rows, parts.shape[1]), 1)) + phase
        xh = (2.0 * x.astype(jnp.float32) + 1.0) / 4096.0 - 1.0
        terms = [parts[(phase * 3 + a) * rows : (phase * 3 + a + 1) * rows] for a in range(3)]
        folded.append(terms[0] + xh * (terms[1] + xh * terms[2]))
    return folded


def together(pieces, join):
    rows = pieces[0].shape[0]
    both = jnp.concatenate(pieces, axis=0)
    high = both.astype(jnp.bfloat16)
    low = (both - high.astype(jnp.float32)).astype(jnp.bfloat16)
    moved = jnp.dot(jnp.concatenate([high, low], axis=0), join, preferred_element_type=jnp.float32)
    moved = moved[: both.shape[0]] + moved[both.shape[0] :]
    return [moved[i * rows : (i + 1) * rows] for i in range(len(pieces))]


def paired(folded, i):
    return jnp.concatenate([phase[:, i * TS : (i + 1) * TS] for phase in folded], axis=1)


def shifted_by(tiles, lag):
    if lag == 0:
        return tiles[1:-1]
    lane = lax.broadcasted_iota(jnp.int32, tiles[0].shape, 1)
    turned = [pltpu.roll(tile, (-lag) % TS, 1) for tile in tiles]
    if lag > 0:
        return [jnp.where(lane < TS - lag, turned[i], turned[i + 1]) for i in range(1, len(tiles) - 1)]
    return [jnp.where(lane < -lag, turned[i - 1], turned[i]) for i in range(1, len(tiles) - 1)]


def main_kernel(planes, weights, science, out, even, odd, held, sems):
    step = pl.program_id(0)
    copies = [
        pltpu.make_async_copy(weights.at[half, pl.ds(part * 96, 96)], held.at[half, pl.ds(part * 96, 96)], sems.at[half, part])
        for half in range(2)
        for part in range(4)
    ]

    def shift(first, buffer):
        near = []
        for phase in range(2):
            tiles = [
                planes[phase, :, pl.ds(pl.multiple_of(jnp.clip(first + i, 0, 15) * TS, TS), TS)] for i in range(-1, TILES + 1)
            ]
            tiles[0] = jnp.where(first > 0, tiles[0], jnp.zeros_like(tiles[0]))
            tiles[-1] = jnp.where(first + TILES < 16, tiles[-1], jnp.zeros_like(tiles[-1]))
            near.append(tiles)
        for index in range(LAGS):
            lag = index - HALF
            for i, tile in enumerate(shifted_by(near[lag % 2], lag // 2)):
                buffer[index, :, i * TS : (i + 1) * TS] = tile

    def multiply(first, buffer):
        pieces = []
        for half in range(2):
            source = buffer[:, half * 48 : half * 48 + WIN, :].reshape(K_MAIN, WIDE)
            parts = jnp.dot(held[half, :, :K_MAIN], source, preferred_element_type=jnp.float32)
            folded = fold(parts, first * TS, SIDE)
            pieces += [paired(folded, i) for i in range(TILES)]
        return pieces

    @pl.when(step == 0)
    def _():
        for copy in copies:
            copy.start()
        shift(0, even)
        for copy in copies:
            copy.wait()

    first = step * 2 * TILES
    shift(first + TILES, odd)
    pieces = multiply(first, even)
    shift(first + 2 * TILES, even)
    pieces += multiply(first + TILES, odd)
    for n, model in enumerate(together(pieces, apart(True))):
        block, half, i = n // (2 * TILES), n // TILES % 2, n % TILES
        at = slice(half * SIDE, (half + 1) * SIDE)
        columns = slice(block * BLOCK + i * 256, block * BLOCK + (i + 1) * 256)
        out[at, columns] = science[at, columns] - model


def rim_kernel(inner, above, below, weights, partial, out, shifted, ends, sems):
    zero = jnp.zeros((EDGE, TS), jnp.bfloat16)
    rows = [pl.ds(0, EDGE), pl.ds(ROWS - EDGE, EDGE)]
    for number in range(2):
        pltpu.make_async_copy(partial.at[rows[number]], ends.at[number], sems.at[0, number]).start()
    pieces = []
    for number, source in enumerate((above, below)):
        keep = inner[number] > 0
        near = []
        for phase in range(2):
            tiles = [source[:, phase * 2048 + i * TS : phase * 2048 + (i + 1) * TS] for i in range(16)]
            near.append([zero] + [jnp.where(keep, tile, zero) for tile in tiles] + [zero])
        for index in range(LAGS):
            lag = index - HALF
            for i, tile in enumerate(shifted_by(near[lag % 2], lag // 2)):
                shifted[number, index, :, i * TS : (i + 1) * TS] = tile
        for first in range(0, 16, 4):
            lags = shifted[number, :, :, first * TS : (first + 4) * TS].reshape(K_EDGE, 4 * TS)
            parts = jnp.dot(weights[number, :, :K_EDGE], lags, preferred_element_type=jnp.float32)
            folded = fold(parts, first * TS, EDGE)
            pieces += [paired(folded, i) for i in range(4)]
    models = together(pieces, apart(True))
    for number in range(2):
        pltpu.make_async_copy(partial.at[rows[number]], ends.at[number], sems.at[0, number]).wait()
        for i in range(16):
            at = slice(i * 256, (i + 1) * 256)
            ends[number, :, at] = ends[number, :, at] - models[number * 16 + i]
        pltpu.make_async_copy(ends.at[number], out.at[rows[number]], sems.at[1, number]).start()
    for number in range(2):
        pltpu.make_async_copy(ends.at[number], out.at[rows[number]], sems.at[1, number]).wait()


def per_device(science, patches, coeffs, tile_owner, tile_patch, tile_offset):
    ccd_id = lax.axis_index("ccd")
    amp_id = lax.axis_index("amp")
    codes = tile_owner[..., 0] | (tile_patch << 4) | (tile_offset[..., 0] << 6) | (tile_offset[..., 1] << 14)
    codes = codes.transpose(1, 0, 2)
    here = jnp.stack([amp_id, ccd_id])

    whole = pl.BlockSpec(memory_space=pltpu.VMEM)
    scalars = pl.BlockSpec(memory_space=pltpu.SMEM)
    send = pl.pallas_call(
        cut_kernel,
        grid=(16 * CAP // CUT,),
        out_shape=pltpu.HBM((16 * CAP, TS, TS), jnp.bfloat16),
        in_specs=[scalars, whole, pl.BlockSpec(memory_space=pl.ANY)],
        out_specs=pl.BlockSpec((CUT, TS, TS), lambda i: (i, 0, 0)),
        scratch_shapes=[
            pltpu.VMEM((4 * 2 * 256, TS), jnp.float32),
            pltpu.VMEM((16, 128), jnp.int32),
            pltpu.SMEM((16, 128), jnp.int32),
            pltpu.SemaphoreType.DMA((4, 2)),
            pltpu.SemaphoreType.DMA,
        ],
        compiler_params=pltpu.CompilerParams(vmem_limit_bytes=10 * MIB),
        name="cut",
    )(here, codes, pltpu.with_memory_space_constraint(patches.reshape(4, 256, 256), pltpu.HBM))
    tiles = lax.all_to_all(send.reshape(16, CAP * TS, TS), "ccd", 0, 0, tiled=True).reshape(16 * CAP, TS, TS)

    order = jnp.arange(32)
    mine = tile_owner[ccd_id, amp_id, :, 0]
    earlier = (mine[:, None] == mine[None, :]) & (order[None, :] < order[:, None])
    slots = mine * CAP + jnp.minimum(jnp.sum(earlier.astype(jnp.int32), axis=1), CAP - 1)

    moments = jnp.einsum("km,kl->ml", coeffs[0], jnp.asarray(basis_table()), precision=lax.Precision.HIGHEST)
    main, edge = pl.pallas_call(
        weights_kernel,
        out_shape=(
            pltpu.HBM((2, 6 * SIDE, K_PAD), jnp.bfloat16),
            jax.ShapeDtypeStruct((2, 6 * EDGE, K_EDGE_PAD), jnp.bfloat16),
        ),
        in_specs=[scalars, whole],
        out_specs=(whole, whole),
        compiler_params=pltpu.CompilerParams(vmem_limit_bytes=10 * MIB),
        cost_estimate=pl.CostEstimate(flops=50_000_000, bytes_accessed=2_000_000, transcendentals=0),
        name="weights",
    )(amp_id.reshape(1), moments)

    planes, top, bottom = pl.pallas_call(
        phase_kernel,
        out_shape=(jax.ShapeDtypeStruct((2, ROWS, 2048), jnp.bfloat16),)
        + (jax.ShapeDtypeStruct((EDGE, 4096), jnp.bfloat16),) * 2,
        in_specs=[scalars, whole],
        out_specs=(whole, whole, whole),
        compiler_params=pltpu.CompilerParams(vmem_limit_bytes=8 * MIB),
        name="phases",
    )(slots, tiles)
    down = [(i, i + 1) for i in range(7)]
    above = lax.ppermute(bottom, "amp", down)
    below = lax.ppermute(top, "amp", [(b, a) for a, b in down])

    columns = pl.BlockSpec((ROWS, 2 * BLOCK), lambda j: (0, j))
    partial = pl.pallas_call(
        main_kernel,
        grid=(4096 // (2 * BLOCK),),
        in_specs=[whole, pl.BlockSpec(memory_space=pl.ANY), columns],
        out_specs=columns,
        scratch_shapes=[pltpu.VMEM((LAGS, ROWS, WIDE), jnp.bfloat16)] * 2
        + [pltpu.VMEM((2, 6 * SIDE, K_PAD), jnp.bfloat16), pltpu.SemaphoreType.DMA((2, 4))],
        out_shape=jax.ShapeDtypeStruct((ROWS, 4096), jnp.float32),
        compiler_params=pltpu.CompilerParams(vmem_limit_bytes=24 * MIB),
        cost_estimate=pl.CostEstimate(flops=11_000_000_000, bytes_accessed=8_000_000, transcendentals=0),
        name="main",
    )(planes, pltpu.with_memory_space_constraint(main, pltpu.HBM), science[0])

    inner = jnp.stack([amp_id > 0, amp_id < 7]).astype(jnp.int32)
    result = pl.pallas_call(
        rim_kernel,
        in_specs=[scalars, whole, whole, whole, pl.BlockSpec(memory_space=pl.ANY)],
        out_specs=pl.BlockSpec(memory_space=pl.ANY),
        scratch_shapes=[
            pltpu.VMEM((2, LAGS, EDGE, 2048), jnp.bfloat16),
            pltpu.VMEM((2, EDGE, 4096), jnp.float32),
            pltpu.SemaphoreType.DMA((2, 2)),
        ],
        out_shape=jax.ShapeDtypeStruct((ROWS, 4096), jnp.float32),
        input_output_aliases={4: 0},
        compiler_params=pltpu.CompilerParams(vmem_limit_bytes=16 * MIB),
        name="rim",
    )(inner, above, below, edge, partial)
    return result[None]


def solution(mesh):
    placed = (
        P("ccd", "amp", None),
        P("ccd", "amp", None, None, None),
        P("ccd", None, None),
        P(),
        P(),
        P(),
    )
    return jax.shard_map(
        per_device, mesh=mesh, in_specs=placed, out_specs=P("ccd", "amp", None), check_vma=False
    )
```

```python
import numpy as np

import jax
import jax.numpy as jnp
import ml_dtypes
from jax import lax
from jax.experimental import pallas as pl
from jax.experimental.pallas import tpu as pltpu
from jax.sharding import PartitionSpec as P

TS = 128
HALF = 10
TAPS = 2 * HALF + 1
CAP = 4
WIDTHS = (1.0, 2.0, 4.0)
DEGREES = (4, 4, 3)
ROWS = 128
SIDE = 64
WIN = 80
EDGE = 16
K_MAIN = TAPS * WIN
K_PAD = 1792
K_EDGE = (TAPS + 1) * EDGE
K_EDGE_PAD = 384
BLOCK = 512
WIDE = BLOCK // 2
TILES = WIDE // TS
LAGS = TAPS + 1
CUT = 16
MIB = 1 << 20


def factor_table():
    offsets = np.arange(-HALF, HALF + 1).astype(np.float64)
    shapes = []
    for width, degree in zip(WIDTHS, DEGREES):
        for power in range(degree + 1):
            profile = np.exp(-offsets * offsets / (2.0 * width * width)) * (offsets / HALF) ** power
            shapes.append(profile / np.sum(np.abs(profile)))
    return np.stack(shapes).astype(np.float32).astype(ml_dtypes.bfloat16).astype(np.float32)


def basis_table():
    factors = factor_table()
    rows = []
    first = 0
    for degree in DEGREES:
        for p in range(degree + 1):
            for q in range(degree + 1 - p):
                grid = np.zeros((TAPS, 128), np.float32)
                grid[:, :TAPS] = factors[first + p][:, None] * factors[first + q][None, :]
                rows.append(grid.reshape(-1))
        first += degree + 1
    return np.stack(rows)


def cut_kernel(here, owners, numbers, offsets, patches, send, halves, *scratch):
    near_owners, near_numbers, near_offsets, listed, table, sems, index_sems, table_sem = scratch
    step = pl.program_id(0)

    @pl.when(step == 0)
    def _():
        copies = [
            pltpu.make_async_copy(
                patches.at[patch, :, pl.ds(side * TS, TS)],
                halves.at[pl.ds((patch * 2 + side) * 256, 256), :],
                sems.at[patch, side],
            )
            for patch in range(4)
            for side in range(2)
        ]
        indices = [
            pltpu.make_async_copy(owners, near_owners, index_sems.at[0]),
            pltpu.make_async_copy(numbers, near_numbers, index_sems.at[1]),
            pltpu.make_async_copy(offsets, near_offsets, index_sems.at[2]),
        ]
        for copy in indices + copies:
            copy.start()
        for copy in indices:
            copy.wait()
        strips = lambda array: array[:, pl.ds(here[0], 1), :].reshape(16, 32)
        owner = strips(near_owners)
        shift = near_offsets[:, pl.ds(here[0], 1)].reshape(16, 2, 32)
        code = owner + strips(near_numbers) * 16 + shift[:, 0] * 64 + shift[:, 1] * 16384
        mine = owner == here[1]
        earlier = lax.broadcasted_iota(jnp.int32, (32, 32), 0) < lax.broadcasted_iota(jnp.int32, (32, 32), 1)
        as_bf16 = lambda mask: mask.astype(jnp.float32).astype(jnp.bfloat16)
        rank = jnp.dot(as_bf16(mine), as_bf16(earlier), preferred_element_type=jnp.float32)
        code = code.astype(jnp.float32)
        lane = lax.broadcasted_iota(jnp.int32, (16, 128), 1)
        total = jnp.zeros((16, 128), jnp.float32)
        for k in range(CAP):
            found = jnp.sum(jnp.where(mine & (rank == k), code, 0.0), axis=1, keepdims=True)
            total = jnp.where(lane == k, found, total)
        listed[...] = total.astype(jnp.int32)
        copy = pltpu.make_async_copy(listed, table, table_sem)
        copy.start()
        copy.wait()
        for copy in copies:
            copy.wait()

    lane = lax.broadcasted_iota(jnp.int32, (TS, TS), 1)

    def tile(slot, carry):
        code = table[step * (CUT // CAP) + slot // CAP, slot % CAP]
        at = ((code >> 4) & 3) * 512 + ((code >> 6) & 255)
        dx = (code >> 14) & 255
        turn = (TS - dx) & (TS - 1)
        low = halves[pl.ds(at, TS), :]
        high = halves[pl.ds(at + 256, TS), :]
        mixed = jnp.where(lane >= dx, low, high).astype(jnp.bfloat16)
        send[slot] = pltpu.roll(mixed, turn, 1)
        return carry

    lax.fori_loop(0, CUT, tile, 0, unroll=4)


def weights_kernel(amp, moments, main, edge):
    first_row = amp[0] * ROWS
    lane = lax.broadcasted_iota(jnp.int32, (SIDE, 128), 1)
    lane16 = lax.broadcasted_iota(jnp.int32, (EDGE, 128), 1)

    def across(rows, members, yh):
        total = jnp.broadcast_to(rows[members[0] : members[0] + 1], (yh.shape[0], 128))
        for power, member in enumerate(members[1:]):
            total = total + (yh if power == 0 else yh * yh) * rows[member : member + 1]
        return pltpu.roll(total, 0, 1, stride=1, stride_axis=0)

    for half in range(2):
        y = (first_row + half * SIDE + lax.broadcasted_iota(jnp.int32, (SIDE, 128), 0)).astype(jnp.float32)
        yh = (2.0 * y + 1.0) / 1024.0 - 1.0
        rim = slice(0, EDGE) if half == 0 else slice(SIDE - EDGE, SIDE)
        lead = 6 if half else -HALF
        rim_lead = EDGE - HALF if half == 0 else SIDE - EDGE + 6 - WIN
        for a, members in enumerate(((0, 2, 5), (1, 4), (3,))):
            held = jnp.zeros((SIDE, 128), jnp.float32)
            held_rim = jnp.zeros((EDGE, 128), jnp.float32)
            for u in range(TAPS):
                moment = moments[:, u * 128 : (u + 1) * 128]
                last = u == TAPS - 1
                group, low = u * WIN // 128, u * WIN % 128
                end = low + WIN
                turned = across(pltpu.roll(moment, (lead + low) % 128, 1), members, yh)
                held = jnp.where((lane >= low) & (lane < end), turned, held)
                at = slice(a * SIDE, (a + 1) * SIDE)
                if end >= 128 or last:
                    main[half, at, group * 128 : (group + 1) * 128] = held.astype(jnp.bfloat16)
                    held = jnp.where(lane < end - 128, turned, 0.0)
                    if last and end > 128:
                        main[half, at, (group + 1) * 128 : (group + 2) * 128] = held.astype(jnp.bfloat16)
                group, low = u * EDGE // 128, u * EDGE % 128
                turned = across(pltpu.roll(moment, (rim_lead + low) % 128, 1), members, yh[rim])
                held_rim = jnp.where((lane16 >= low) & (lane16 < low + EDGE), turned, held_rim)
                if low + EDGE == 128 or last:
                    at = slice(a * EDGE, (a + 1) * EDGE)
                    edge[half, at, group * 128 : (group + 1) * 128] = held_rim.astype(jnp.bfloat16)
                    held_rim = jnp.zeros((EDGE, 128), jnp.float32)
        edge[half, 3 * EDGE :, :] = pltpu.roll(edge[half, : 3 * EDGE, :], EDGE, 1)


def apart(transposed):
    wide, narrow = (1, 0) if transposed else (0, 1)
    column = lax.broadcasted_iota(jnp.int32, (256, 256), wide)
    place = lax.broadcasted_iota(jnp.int32, (256, 256), narrow)
    home = jnp.where(place < TS, 2 * place, 2 * place - 255)
    return (column == home).astype(jnp.float32).astype(jnp.bfloat16)


def phase_kernel(slots, tiles, planes, top, bottom):
    split = apart(False)
    for pair in range(16):
        both = jnp.concatenate([tiles[slots[2 * pair]], tiles[slots[2 * pair + 1]]], axis=1)
        moved = jnp.dot(both, split, preferred_element_type=jnp.float32).astype(jnp.bfloat16)
        for phase in range(2):
            piece = moved[:, phase * TS : (phase + 1) * TS]
            planes[phase, :, pair * TS : (pair + 1) * TS] = piece
            at = slice(phase * 2048 + pair * TS, phase * 2048 + (pair + 1) * TS)
            top[:, at] = piece[:EDGE]
            bottom[:, at] = piece[TS - EDGE :]


def fold(parts, first, rows):
    folded = []
    for phase, part in enumerate(parts):
        x = 2 * (first + lax.broadcasted_iota(jnp.int32, (rows, part.shape[1]), 1)) + phase
        xh = (2.0 * x.astype(jnp.float32) + 1.0) / 4096.0 - 1.0
        terms = [part[a * rows : (a + 1) * rows] for a in range(3)]
        folded.append(terms[0] + xh * (terms[1] + xh * terms[2]))
    return folded


def product(weights, lags):
    return [
        jnp.dot(
            weights,
            lags[phase : phase + TAPS].reshape(weights.shape[1], lags.shape[2]),
            preferred_element_type=jnp.float32,
        )
        for phase in range(2)
    ]


def together(pieces, join):
    rows = pieces[0].shape[0]
    both = jnp.concatenate(pieces, axis=0)
    high = both.astype(jnp.bfloat16)
    low = (both - high.astype(jnp.float32)).astype(jnp.bfloat16)
    moved = jnp.dot(jnp.concatenate([high, low], axis=0), join, preferred_element_type=jnp.float32)
    moved = moved[: both.shape[0]] + moved[both.shape[0] :]
    return [moved[i * rows : (i + 1) * rows] for i in range(len(pieces))]


def paired(folded, i):
    return jnp.concatenate([phase[:, i * TS : (i + 1) * TS] for phase in folded], axis=1)


def shifted_by(tiles, lag):
    if lag == 0:
        return tiles[1:-1]
    lane = lax.broadcasted_iota(jnp.int32, tiles[0].shape, 1)
    if lag > 0:
        mixed = [jnp.where(lane >= lag, tiles[i], tiles[i + 1]) for i in range(1, len(tiles) - 1)]
    else:
        mixed = [jnp.where(lane < TS + lag, tiles[i], tiles[i - 1]) for i in range(1, len(tiles) - 1)]
    return [pltpu.roll(tile, (-lag) % TS, 1) for tile in mixed]


def main_kernel(planes, weights, science, out, even, odd, held, sems):
    step = pl.program_id(0)
    copies = [
        pltpu.make_async_copy(weights.at[half, pl.ds(part * 48, 48)], held.at[half, pl.ds(part * 48, 48)], sems.at[half, part])
        for half in range(2)
        for part in range(4)
    ]
    def shift(first, buffer):
        near = []
        for phase in range(2):
            tiles = [
                planes[phase, :, pl.ds(pl.multiple_of(jnp.clip(first + i, 0, 15) * TS, TS), TS)] for i in range(-1, TILES + 1)
            ]
            tiles[0] = jnp.where(first > 0, tiles[0], jnp.zeros_like(tiles[0]))
            tiles[-1] = jnp.where(first + TILES < 16, tiles[-1], jnp.zeros_like(tiles[-1]))
            near.append(tiles)
        for index in range(LAGS):
            lag = index - HALF
            for i, tile in enumerate(shifted_by(near[lag % 2], lag // 2)):
                buffer[index, :, i * TS : (i + 1) * TS] = tile

    def multiply(first, buffer):
        pieces = []
        for half in range(2):
            parts = product(held[half, :, :K_MAIN], buffer[:, half * 48 : half * 48 + WIN, :])
            folded = fold(parts, first * TS, SIDE)
            pieces += [paired(folded, i) for i in range(TILES)]
        return pieces

    @pl.when(step == 0)
    def _():
        for copy in copies:
            copy.start()
        shift(0, even)
        for copy in copies:
            copy.wait()

    first = step * 2 * TILES
    shift(first + TILES, odd)
    pieces = multiply(first, even)
    shift(first + 2 * TILES, even)
    pieces += multiply(first + TILES, odd)
    for n, model in enumerate(together(pieces, apart(True))):
        block, half, i = n // (2 * TILES), n // TILES % 2, n % TILES
        at = slice(half * SIDE, (half + 1) * SIDE)
        columns = slice(block * BLOCK + i * 256, block * BLOCK + (i + 1) * 256)
        out[at, columns] = science[at, columns] - model


def rim_kernel(inner, above, below, weights, partial, out, shifted, ends, sems):
    zero = jnp.zeros((EDGE, TS), jnp.bfloat16)
    rows = [pl.ds(0, EDGE), pl.ds(ROWS - EDGE, EDGE)]
    for number in range(2):
        pltpu.make_async_copy(partial.at[rows[number]], ends.at[number], sems.at[0, number]).start()
    pieces = []
    for number, source in enumerate((above, below)):
        keep = inner[number] > 0
        near = []
        for phase in range(2):
            tiles = [source[:, phase * 2048 + i * TS : phase * 2048 + (i + 1) * TS] for i in range(16)]
            near.append([zero] + [jnp.where(keep, tile, zero) for tile in tiles] + [zero])
        for index in range(LAGS):
            lag = index - HALF
            for i, tile in enumerate(shifted_by(near[lag % 2], lag // 2)):
                shifted[number, index, :, i * TS : (i + 1) * TS] = tile
        for first in range(0, 16, 4):
            lags = shifted[number, :, :, first * TS : (first + 4) * TS].reshape(K_EDGE, 4 * TS)
            parts = jnp.dot(weights[number, :, :K_EDGE], lags, preferred_element_type=jnp.float32)
            parts = [parts[: 3 * EDGE], parts[3 * EDGE :]]
            folded = fold(parts, first * TS, EDGE)
            pieces += [paired(folded, i) for i in range(4)]
    models = together(pieces, apart(True))
    for number in range(2):
        pltpu.make_async_copy(partial.at[rows[number]], ends.at[number], sems.at[0, number]).wait()
        for i in range(16):
            at = slice(i * 256, (i + 1) * 256)
            ends[number, :, at] = ends[number, :, at] - models[number * 16 + i]
        pltpu.make_async_copy(ends.at[number], out.at[rows[number]], sems.at[1, number]).start()
    for number in range(2):
        pltpu.make_async_copy(ends.at[number], out.at[rows[number]], sems.at[1, number]).wait()


def per_device(science, patches, coeffs, tile_owner, tile_patch, tile_offset):
    ccd_id = lax.axis_index("ccd")
    amp_id = lax.axis_index("amp")
    here = jnp.stack([amp_id, ccd_id])

    far = lambda array: pltpu.with_memory_space_constraint(array, pltpu.HBM)
    whole = pl.BlockSpec(memory_space=pltpu.VMEM)
    scalars = pl.BlockSpec(memory_space=pltpu.SMEM)
    send = pl.pallas_call(
        cut_kernel,
        grid=(16 * CAP // CUT,),
        out_shape=pltpu.HBM((16 * CAP, TS, TS), jnp.bfloat16),
        in_specs=[scalars] + [pl.BlockSpec(memory_space=pl.ANY)] * 4,
        out_specs=pl.BlockSpec((CUT, TS, TS), lambda i: (i, 0, 0)),
        scratch_shapes=[
            pltpu.VMEM((4 * 2 * 256, TS), jnp.float32),
            pltpu.VMEM((16, 8, 32), jnp.int32),
            pltpu.VMEM((16, 8, 32), jnp.int32),
            pltpu.VMEM((16, 8, 2, 32), jnp.int32),
            pltpu.VMEM((16, 128), jnp.int32),
            pltpu.SMEM((16, 128), jnp.int32),
            pltpu.SemaphoreType.DMA((4, 2)),
            pltpu.SemaphoreType.DMA((3,)),
            pltpu.SemaphoreType.DMA,
        ],
        compiler_params=pltpu.CompilerParams(vmem_limit_bytes=10 * MIB),
        name="cut",
    )(
        here,
        far(tile_owner.reshape(16, 8, 32)),
        far(tile_patch),
        far(tile_offset.transpose(0, 1, 3, 2)),
        far(patches.reshape(4, 256, 256)),
    )
    tiles = lax.all_to_all(send.reshape(16, CAP * TS, TS), "ccd", 0, 0, tiled=True).reshape(16 * CAP, TS, TS)

    order = jnp.arange(32)
    mine = tile_owner[ccd_id, amp_id, :, 0]
    earlier = (mine[:, None] == mine[None, :]) & (order[None, :] < order[:, None])
    slots = mine * CAP + jnp.minimum(jnp.sum(earlier.astype(jnp.int32), axis=1), CAP - 1)

    moments = jnp.einsum("km,kl->ml", coeffs[0], jnp.asarray(basis_table()), precision=lax.Precision.HIGHEST)
    main, edge = pl.pallas_call(
        weights_kernel,
        out_shape=(
            pltpu.HBM((2, 3 * SIDE, K_PAD), jnp.bfloat16),
            jax.ShapeDtypeStruct((2, 6 * EDGE, K_EDGE_PAD), jnp.bfloat16),
        ),
        in_specs=[scalars, whole],
        out_specs=(whole, whole),
        compiler_params=pltpu.CompilerParams(vmem_limit_bytes=10 * MIB),
        cost_estimate=pl.CostEstimate(flops=50_000_000, bytes_accessed=2_000_000, transcendentals=0),
        name="weights",
    )(amp_id.reshape(1), moments)

    planes, top, bottom = pl.pallas_call(
        phase_kernel,
        out_shape=(jax.ShapeDtypeStruct((2, ROWS, 2048), jnp.bfloat16),)
        + (jax.ShapeDtypeStruct((EDGE, 4096), jnp.bfloat16),) * 2,
        in_specs=[scalars, whole],
        out_specs=(whole, whole, whole),
        compiler_params=pltpu.CompilerParams(vmem_limit_bytes=8 * MIB),
        name="phases",
    )(slots, tiles)
    down = [(i, i + 1) for i in range(7)]
    above = lax.ppermute(bottom, "amp", down)
    below = lax.ppermute(top, "amp", [(b, a) for a, b in down])

    columns = pl.BlockSpec((ROWS, 2 * BLOCK), lambda j: (0, j))
    partial = pl.pallas_call(
        main_kernel,
        grid=(4096 // (2 * BLOCK),),
        in_specs=[whole, pl.BlockSpec(memory_space=pl.ANY), columns],
        out_specs=columns,
        scratch_shapes=[pltpu.VMEM((LAGS, ROWS, WIDE), jnp.bfloat16)] * 2
        + [pltpu.VMEM((2, 3 * SIDE, K_PAD), jnp.bfloat16), pltpu.SemaphoreType.DMA((2, 4))],
        out_shape=jax.ShapeDtypeStruct((ROWS, 4096), jnp.float32),
        compiler_params=pltpu.CompilerParams(vmem_limit_bytes=24 * MIB),
        cost_estimate=pl.CostEstimate(flops=11_000_000_000, bytes_accessed=8_000_000, transcendentals=0),
        name="main",
    )(planes, pltpu.with_memory_space_constraint(main, pltpu.HBM), science[0])

    inner = jnp.stack([amp_id > 0, amp_id < 7]).astype(jnp.int32)
    result = pl.pallas_call(
        rim_kernel,
        in_specs=[scalars, whole, whole, whole, pl.BlockSpec(memory_space=pl.ANY)],
        out_specs=pl.BlockSpec(memory_space=pl.ANY),
        scratch_shapes=[
            pltpu.VMEM((2, LAGS, EDGE, 2048), jnp.bfloat16),
            pltpu.VMEM((2, EDGE, 4096), jnp.float32),
            pltpu.SemaphoreType.DMA((2, 2)),
        ],
        out_shape=jax.ShapeDtypeStruct((ROWS, 4096), jnp.float32),
        input_output_aliases={4: 0},
        compiler_params=pltpu.CompilerParams(vmem_limit_bytes=16 * MIB),
        name="rim",
    )(inner, above, below, edge, partial)
    return result[None]


def solution(mesh):
    placed = (
        P("ccd", "amp", None),
        P("ccd", "amp", None, None, None),
        P("ccd", None, None),
        P(),
        P(),
        P(),
    )
    return jax.shard_map(
        per_device, mesh=mesh, in_specs=placed, out_specs=P("ccd", "amp", None), check_vma=False
    )
```

```python
import numpy as np

import jax
import jax.numpy as jnp
import ml_dtypes
from jax import lax
from jax.experimental import pallas as pl
from jax.experimental.pallas import tpu as pltpu
from jax.sharding import PartitionSpec as P

TS = 128
HALF = 10
TAPS = 2 * HALF + 1
CAP = 4
WIDTHS = (1.0, 2.0, 4.0)
DEGREES = (4, 4, 3)
ROWS = 128
SIDE = 64
WIN = 80
EDGE = 16
K_MAIN = TAPS * WIN
K_PAD = 1792
K_EDGE = (TAPS + 1) * EDGE
K_EDGE_PAD = 384
BLOCK = 512
WIDE = BLOCK // 2
TILES = WIDE // TS
LAGS = TAPS + 1
CUT = 32
MIB = 1 << 20


def factor_table():
    offsets = np.arange(-HALF, HALF + 1).astype(np.float64)
    shapes = []
    for width, degree in zip(WIDTHS, DEGREES):
        for power in range(degree + 1):
            profile = np.exp(-offsets * offsets / (2.0 * width * width)) * (offsets / HALF) ** power
            shapes.append(profile / np.sum(np.abs(profile)))
    return np.stack(shapes).astype(np.float32).astype(ml_dtypes.bfloat16).astype(np.float32)


def basis_table():
    factors = factor_table()
    rows = []
    first = 0
    for degree in DEGREES:
        for p in range(degree + 1):
            for q in range(degree + 1 - p):
                grid = np.zeros((TAPS, 128), np.float32)
                grid[:, :TAPS] = factors[first + p][:, None] * factors[first + q][None, :]
                rows.append(grid.reshape(-1))
        first += degree + 1
    return np.stack(rows)


def cut_kernel(here, owners, numbers, offsets, patches, send, halves, *scratch):
    near_owners, near_numbers, near_offsets, listed, table, sems, index_sems, table_sem = scratch
    step = pl.program_id(0)

    @pl.when(step == 0)
    def _():
        copies = [
            pltpu.make_async_copy(
                patches.at[patch, :, pl.ds(side * TS, TS)],
                halves.at[pl.ds((patch * 2 + side) * 256, 256), :],
                sems.at[patch, side],
            )
            for patch in range(4)
            for side in range(2)
        ]
        indices = [
            pltpu.make_async_copy(owners, near_owners, index_sems.at[0]),
            pltpu.make_async_copy(numbers, near_numbers, index_sems.at[1]),
            pltpu.make_async_copy(offsets, near_offsets, index_sems.at[2]),
        ]
        for copy in indices + copies:
            copy.start()
        for copy in indices:
            copy.wait()
        strips = lambda array: array[:, pl.ds(here[0], 1), :].reshape(16, 32)
        owner = strips(near_owners)
        shift = near_offsets[:, pl.ds(here[0], 1)].reshape(16, 2, 32)
        code = owner + strips(near_numbers) * 16 + shift[:, 0] * 64 + shift[:, 1] * 16384
        mine = owner == here[1]
        earlier = lax.broadcasted_iota(jnp.int32, (32, 32), 0) < lax.broadcasted_iota(jnp.int32, (32, 32), 1)
        as_bf16 = lambda mask: mask.astype(jnp.float32).astype(jnp.bfloat16)
        rank = jnp.dot(as_bf16(mine), as_bf16(earlier), preferred_element_type=jnp.float32)
        code = code.astype(jnp.float32)
        lane = lax.broadcasted_iota(jnp.int32, (16, 128), 1)
        total = jnp.zeros((16, 128), jnp.float32)
        for k in range(CAP):
            found = jnp.sum(jnp.where(mine & (rank == k), code, 0.0), axis=1, keepdims=True)
            total = jnp.where(lane == k, found, total)
        listed[...] = total.astype(jnp.int32)
        copy = pltpu.make_async_copy(listed, table, table_sem)
        copy.start()
        copy.wait()
        for copy in copies:
            copy.wait()

    lane = lax.broadcasted_iota(jnp.int32, (TS, TS), 1)

    def tile(slot, carry):
        code = table[step * (CUT // CAP) + slot // CAP, slot % CAP]
        at = ((code >> 4) & 3) * 512 + ((code >> 6) & 255)
        dx = (code >> 14) & 255
        turn = (TS - dx) & (TS - 1)
        low = halves[pl.ds(at, TS), :]
        high = halves[pl.ds(at + 256, TS), :]
        mixed = jnp.where(lane >= dx, low, high).astype(jnp.bfloat16)
        send[slot] = pltpu.roll(mixed, turn, 1)
        return carry

    lax.fori_loop(0, CUT, tile, 0, unroll=CUT)


def weights_kernel(amp, moments, *outs):
    main, edge = outs[:6], outs[6]
    first_row = amp[0] * ROWS
    lane = lax.broadcasted_iota(jnp.int32, (SIDE, 128), 1)
    lane16 = lax.broadcasted_iota(jnp.int32, (EDGE, 128), 1)

    def across(rows, members, yh):
        total = jnp.broadcast_to(rows[members[0] : members[0] + 1], (yh.shape[0], 128))
        for power, member in enumerate(members[1:]):
            total = total + (yh if power == 0 else yh * yh) * rows[member : member + 1]
        return pltpu.roll(total, 0, 1, stride=1, stride_axis=0)

    for half in range(2):
        y = (first_row + half * SIDE + lax.broadcasted_iota(jnp.int32, (SIDE, 128), 0)).astype(jnp.float32)
        yh = (2.0 * y + 1.0) / 1024.0 - 1.0
        rim = slice(0, EDGE) if half == 0 else slice(SIDE - EDGE, SIDE)
        lead = 6 if half else -HALF
        rim_lead = EDGE - HALF if half == 0 else SIDE - EDGE + 6 - WIN
        for a, members in enumerate(((0, 2, 5), (1, 4), (3,))):
            held = jnp.zeros((SIDE, 128), jnp.float32)
            held_rim = jnp.zeros((EDGE, 128), jnp.float32)
            for u in range(TAPS):
                moment = moments[:, u * 128 : (u + 1) * 128]
                last = u == TAPS - 1
                group, low = u * WIN // 128, u * WIN % 128
                end = low + WIN
                turned = across(pltpu.roll(moment, (lead + low) % 128, 1), members, yh)
                held = jnp.where((lane >= low) & (lane < end), turned, held)
                if end >= 128 or last:
                    main[half * 3 + a][:, group * 128 : (group + 1) * 128] = held.astype(jnp.bfloat16)
                    held = jnp.where(lane < end - 128, turned, 0.0)
                    if last and end > 128:
                        main[half * 3 + a][:, (group + 1) * 128 : (group + 2) * 128] = held.astype(jnp.bfloat16)
                group, low = u * EDGE // 128, u * EDGE % 128
                turned = across(pltpu.roll(moment, (rim_lead + low) % 128, 1), members, yh[rim])
                held_rim = jnp.where((lane16 >= low) & (lane16 < low + EDGE), turned, held_rim)
                if low + EDGE == 128 or last:
                    at = slice(a * EDGE, (a + 1) * EDGE)
                    edge[half, at, group * 128 : (group + 1) * 128] = held_rim.astype(jnp.bfloat16)
                    held_rim = jnp.zeros((EDGE, 128), jnp.float32)
        edge[half, 3 * EDGE :, :] = pltpu.roll(edge[half, : 3 * EDGE, :], EDGE, 1)


def apart(transposed):
    wide, narrow = (1, 0) if transposed else (0, 1)
    column = lax.broadcasted_iota(jnp.int32, (256, 256), wide)
    place = lax.broadcasted_iota(jnp.int32, (256, 256), narrow)
    home = jnp.where(place < TS, 2 * place, 2 * place - 255)
    return (column == home).astype(jnp.float32).astype(jnp.bfloat16)


def phase_kernel(slots, tiles, far_weights, planes, top, bottom, near_weights, sem):
    copy = pltpu.make_async_copy(far_weights, near_weights, sem)
    copy.start()
    split = apart(False)
    for pair in range(16):
        both = jnp.concatenate([tiles[slots[2 * pair]], tiles[slots[2 * pair + 1]]], axis=1)
        moved = jnp.dot(both, split, preferred_element_type=jnp.float32).astype(jnp.bfloat16)
        for phase in range(2):
            piece = moved[:, phase * TS : (phase + 1) * TS]
            planes[phase, :, pair * TS : (pair + 1) * TS] = piece
            at = slice(phase * 2048 + pair * TS, phase * 2048 + (pair + 1) * TS)
            top[:, at] = piece[:EDGE]
            bottom[:, at] = piece[TS - EDGE :]
    copy.wait()


def fold(parts, first, rows):
    folded = []
    for phase, part in enumerate(parts):
        x = 2 * (first + lax.broadcasted_iota(jnp.int32, (rows, part.shape[1]), 1)) + phase
        xh = (2.0 * x.astype(jnp.float32) + 1.0) / 4096.0 - 1.0
        terms = [part[a * rows : (a + 1) * rows] for a in range(3)]
        folded.append(terms[0] + xh * (terms[1] + xh * terms[2]))
    return folded


def product(weights, lags):
    return [
        jnp.dot(
            weights,
            lags[phase : phase + TAPS].reshape(weights.shape[1], lags.shape[2]),
            preferred_element_type=jnp.float32,
        )
        for phase in range(2)
    ]


def together(pieces, join):
    rows = pieces[0].shape[0]
    both = jnp.concatenate(pieces, axis=0)
    high = both.astype(jnp.bfloat16)
    low = (both - high.astype(jnp.float32)).astype(jnp.bfloat16)
    moved = jnp.dot(jnp.concatenate([high, low], axis=0), join, preferred_element_type=jnp.float32)
    moved = moved[: both.shape[0]] + moved[both.shape[0] :]
    return [moved[i * rows : (i + 1) * rows] for i in range(len(pieces))]


def paired(folded, i):
    return jnp.concatenate([phase[:, i * TS : (i + 1) * TS] for phase in folded], axis=1)


def shifted_by(tiles, lag):
    if lag == 0:
        return tiles[1:-1]
    lane = lax.broadcasted_iota(jnp.int32, tiles[0].shape, 1)
    if lag > 0:
        mixed = [jnp.where(lane >= lag, tiles[i], tiles[i + 1]) for i in range(1, len(tiles) - 1)]
    else:
        mixed = [jnp.where(lane < TS + lag, tiles[i], tiles[i - 1]) for i in range(1, len(tiles) - 1)]
    return [pltpu.roll(tile, (-lag) % TS, 1) for tile in mixed]


def main_kernel(planes, *refs):
    weights, (science, out, even, odd) = refs[:6], refs[6:]
    step = pl.program_id(0)

    def shift(first, buffer):
        near = []
        for phase in range(2):
            tiles = [
                planes[phase, :, pl.ds(pl.multiple_of(jnp.clip(first + i, 0, 15) * TS, TS), TS)] for i in range(-1, TILES + 1)
            ]
            tiles[0] = jnp.where(first > 0, tiles[0], jnp.zeros_like(tiles[0]))
            tiles[-1] = jnp.where(first + TILES < 16, tiles[-1], jnp.zeros_like(tiles[-1]))
            near.append(tiles)
        for index in range(LAGS):
            lag = index - HALF
            for i, tile in enumerate(shifted_by(near[lag % 2], lag // 2)):
                buffer[index, :, i * TS : (i + 1) * TS] = tile

    def multiply(first, buffer):
        pieces = []
        for half in range(2):
            members = [weights[half * 3 + a][:, :K_MAIN] for a in range(3)]
            parts = product(jnp.concatenate(members, axis=0), buffer[:, half * 48 : half * 48 + WIN, :])
            folded = fold(parts, first * TS, SIDE)
            pieces += [paired(folded, i) for i in range(TILES)]
        return pieces

    @pl.when(step == 0)
    def _():
        shift(0, even)

    first = step * 2 * TILES
    shift(first + TILES, odd)
    pieces = multiply(first, even)
    shift(first + 2 * TILES, even)
    pieces += multiply(first + TILES, odd)
    for n, model in enumerate(together(pieces, apart(True))):
        block, half, i = n // (2 * TILES), n // TILES % 2, n % TILES
        at = slice(half * SIDE, (half + 1) * SIDE)
        columns = slice(block * BLOCK + i * 256, block * BLOCK + (i + 1) * 256)
        out[at, columns] = science[at, columns] - model


def rim_kernel(inner, above, below, weights, partial, out, shifted, ends, sems):
    zero = jnp.zeros((EDGE, TS), jnp.bfloat16)
    rows = [pl.ds(0, EDGE), pl.ds(ROWS - EDGE, EDGE)]
    for number in range(2):
        pltpu.make_async_copy(partial.at[rows[number]], ends.at[number], sems.at[0, number]).start()
    pieces = []
    for number, source in enumerate((above, below)):
        keep = inner[number] > 0
        near = []
        for phase in range(2):
            tiles = [source[:, phase * 2048 + i * TS : phase * 2048 + (i + 1) * TS] for i in range(16)]
            near.append([zero] + [jnp.where(keep, tile, zero) for tile in tiles] + [zero])
        for index in range(LAGS):
            lag = index - HALF
            for i, tile in enumerate(shifted_by(near[lag % 2], lag // 2)):
                shifted[number, index, :, i * TS : (i + 1) * TS] = tile
        for first in range(0, 16, 4):
            lags = shifted[number, :, :, first * TS : (first + 4) * TS].reshape(K_EDGE, 4 * TS)
            parts = jnp.dot(weights[number, :, :K_EDGE], lags, preferred_element_type=jnp.float32)
            parts = [parts[: 3 * EDGE], parts[3 * EDGE :]]
            folded = fold(parts, first * TS, EDGE)
            pieces += [paired(folded, i) for i in range(4)]
    models = together(pieces, apart(True))
    for number in range(2):
        pltpu.make_async_copy(partial.at[rows[number]], ends.at[number], sems.at[0, number]).wait()
        for i in range(16):
            at = slice(i * 256, (i + 1) * 256)
            ends[number, :, at] = ends[number, :, at] - models[number * 16 + i]
        pltpu.make_async_copy(ends.at[number], out.at[rows[number]], sems.at[1, number]).start()
    for number in range(2):
        pltpu.make_async_copy(ends.at[number], out.at[rows[number]], sems.at[1, number]).wait()


def per_device(science, patches, coeffs, tile_owner, tile_patch, tile_offset):
    ccd_id = lax.axis_index("ccd")
    amp_id = lax.axis_index("amp")
    here = jnp.stack([amp_id, ccd_id])

    far = lambda array: pltpu.with_memory_space_constraint(array, pltpu.HBM)
    whole = pl.BlockSpec(memory_space=pltpu.VMEM)
    scalars = pl.BlockSpec(memory_space=pltpu.SMEM)
    send = pl.pallas_call(
        cut_kernel,
        grid=(16 * CAP // CUT,),
        out_shape=pltpu.HBM((16 * CAP, TS, TS), jnp.bfloat16),
        in_specs=[scalars] + [pl.BlockSpec(memory_space=pl.ANY)] * 4,
        out_specs=pl.BlockSpec((CUT, TS, TS), lambda i: (i, 0, 0)),
        scratch_shapes=[
            pltpu.VMEM((4 * 2 * 256, TS), jnp.float32),
            pltpu.VMEM((16, 8, 32), jnp.int32),
            pltpu.VMEM((16, 8, 32), jnp.int32),
            pltpu.VMEM((16, 8, 2, 32), jnp.int32),
            pltpu.VMEM((16, 128), jnp.int32),
            pltpu.SMEM((16, 128), jnp.int32),
            pltpu.SemaphoreType.DMA((4, 2)),
            pltpu.SemaphoreType.DMA((3,)),
            pltpu.SemaphoreType.DMA,
        ],
        compiler_params=pltpu.CompilerParams(vmem_limit_bytes=10 * MIB),
        name="cut",
    )(
        here,
        far(tile_owner.reshape(16, 8, 32)),
        far(tile_patch),
        far(tile_offset.transpose(0, 1, 3, 2)),
        far(patches.reshape(4, 256, 256)),
    )
    tiles = lax.all_to_all(send.reshape(16, CAP * TS, TS), "ccd", 0, 0, tiled=True).reshape(16 * CAP, TS, TS)

    order = jnp.arange(32)
    mine = tile_owner[ccd_id, amp_id, :, 0]
    earlier = (mine[:, None] == mine[None, :]) & (order[None, :] < order[:, None])
    slots = mine * CAP + jnp.minimum(jnp.sum(earlier.astype(jnp.int32), axis=1), CAP - 1)

    moments = jnp.einsum("km,kl->ml", coeffs[0], jnp.asarray(basis_table()), precision=lax.Precision.HIGHEST)
    *main, edge = pl.pallas_call(
        weights_kernel,
        out_shape=(
            *([jax.ShapeDtypeStruct((SIDE, K_PAD), jnp.bfloat16)] * 5),
            pltpu.HBM((SIDE, K_PAD), jnp.bfloat16),
            jax.ShapeDtypeStruct((2, 6 * EDGE, K_EDGE_PAD), jnp.bfloat16),
        ),
        in_specs=[scalars, whole],
        out_specs=(whole,) * 7,
        compiler_params=pltpu.CompilerParams(vmem_limit_bytes=10 * MIB),
        cost_estimate=pl.CostEstimate(flops=50_000_000, bytes_accessed=2_000_000, transcendentals=0),
        name="weights",
    )(amp_id.reshape(1), moments)

    planes, top, bottom, main[5] = pl.pallas_call(
        phase_kernel,
        out_shape=(
            jax.ShapeDtypeStruct((2, ROWS, 2048), jnp.bfloat16),
            *([jax.ShapeDtypeStruct((EDGE, 4096), jnp.bfloat16)] * 2),
            jax.ShapeDtypeStruct((SIDE, K_PAD), jnp.bfloat16),
        ),
        in_specs=[scalars, whole, pl.BlockSpec(memory_space=pl.ANY)],
        out_specs=(whole,) * 4,
        scratch_shapes=[pltpu.SemaphoreType.DMA],
        compiler_params=pltpu.CompilerParams(vmem_limit_bytes=8 * MIB),
        name="phases",
    )(slots, tiles, far(main[5]))
    down = [(i, i + 1) for i in range(7)]
    above = lax.ppermute(bottom, "amp", down)
    below = lax.ppermute(top, "amp", [(b, a) for a, b in down])

    columns = pl.BlockSpec((ROWS, 2 * BLOCK), lambda j: (0, j))
    partial = pl.pallas_call(
        main_kernel,
        grid=(4096 // (2 * BLOCK),),
        in_specs=[whole] * 7 + [columns],
        out_specs=columns,
        scratch_shapes=[pltpu.VMEM((LAGS, ROWS, WIDE), jnp.bfloat16)] * 2,
        out_shape=jax.ShapeDtypeStruct((ROWS, 4096), jnp.float32),
        compiler_params=pltpu.CompilerParams(vmem_limit_bytes=12 * MIB),
        cost_estimate=pl.CostEstimate(flops=11_000_000_000, bytes_accessed=8_000_000, transcendentals=0),
        name="main",
    )(planes, *main, science[0])

    inner = jnp.stack([amp_id > 0, amp_id < 7]).astype(jnp.int32)
    result = pl.pallas_call(
        rim_kernel,
        in_specs=[scalars, whole, whole, whole, pl.BlockSpec(memory_space=pl.ANY)],
        out_specs=pl.BlockSpec(memory_space=pl.ANY),
        scratch_shapes=[
            pltpu.VMEM((2, LAGS, EDGE, 2048), jnp.bfloat16),
            pltpu.VMEM((2, EDGE, 4096), jnp.float32),
            pltpu.SemaphoreType.DMA((2, 2)),
        ],
        out_shape=jax.ShapeDtypeStruct((ROWS, 4096), jnp.float32),
        input_output_aliases={4: 0},
        compiler_params=pltpu.CompilerParams(vmem_limit_bytes=10 * MIB),
        name="rim",
    )(inner, above, below, edge, partial)
    return result[None]


def solution(mesh):
    placed = (
        P("ccd", "amp", None),
        P("ccd", "amp", None, None, None),
        P("ccd", None, None),
        P(),
        P(),
        P(),
    )
    return jax.shard_map(
        per_device, mesh=mesh, in_specs=placed, out_specs=P("ccd", "amp", None), check_vma=False
    )
```

```python
import numpy as np

import jax
import jax.numpy as jnp
import ml_dtypes
from jax import lax
from jax.experimental import pallas as pl
from jax.experimental.pallas import tpu as pltpu
from jax.sharding import PartitionSpec as P

TS = 128
HALF = 10
TAPS = 2 * HALF + 1
CAP = 4
WIDTHS = (1.0, 2.0, 4.0)
DEGREES = (4, 4, 3)
ROWS = 128
SIDE = 64
WIN = 80
EDGE = 16
K_MAIN = TAPS * WIN
K_PAD = 1792
K_EDGE = (TAPS + 1) * EDGE
K_EDGE_PAD = 384
BLOCK = 512
WIDE = BLOCK // 2
TILES = WIDE // TS
LAGS = TAPS + 1
CUT = 32
MIB = 1 << 20


def factor_table():
    offsets = np.arange(-HALF, HALF + 1).astype(np.float64)
    shapes = []
    for width, degree in zip(WIDTHS, DEGREES):
        for power in range(degree + 1):
            profile = np.exp(-offsets * offsets / (2.0 * width * width)) * (offsets / HALF) ** power
            shapes.append(profile / np.sum(np.abs(profile)))
    return np.stack(shapes).astype(np.float32).astype(ml_dtypes.bfloat16).astype(np.float32)


def basis_table():
    factors = factor_table()
    rows = []
    first = 0
    for degree in DEGREES:
        for p in range(degree + 1):
            for q in range(degree + 1 - p):
                grid = np.zeros((TAPS, 128), np.float32)
                grid[:, :TAPS] = factors[first + p][:, None] * factors[first + q][None, :]
                rows.append(grid.reshape(-1))
        first += degree + 1
    return np.stack(rows)


def cut_kernel(here, owners, numbers, offsets, patches, send, halves, *scratch):
    near_owners, near_numbers, near_offsets, listed, table, sems, index_sems, table_sem = scratch
    step = pl.program_id(0)

    @pl.when(step == 0)
    def _():
        copies = [
            pltpu.make_async_copy(
                patches.at[patch, :, pl.ds(side * TS, TS)],
                halves.at[pl.ds((patch * 2 + side) * 256, 256), :],
                sems.at[patch, side],
            )
            for patch in range(4)
            for side in range(2)
        ]
        indices = [
            pltpu.make_async_copy(owners, near_owners, index_sems.at[0]),
            pltpu.make_async_copy(numbers, near_numbers, index_sems.at[1]),
            pltpu.make_async_copy(offsets, near_offsets, index_sems.at[2]),
        ]
        for copy in indices + copies:
            copy.start()
        for copy in indices:
            copy.wait()
        strips = lambda array: array[:, pl.ds(here[0], 1), :].reshape(16, 32)
        owner = strips(near_owners)
        shift = near_offsets[:, pl.ds(here[0], 1)].reshape(16, 2, 32)
        code = owner + strips(near_numbers) * 16 + shift[:, 0] * 64 + shift[:, 1] * 16384
        mine = owner == here[1]
        earlier = lax.broadcasted_iota(jnp.int32, (32, 32), 0) < lax.broadcasted_iota(jnp.int32, (32, 32), 1)
        as_bf16 = lambda mask: mask.astype(jnp.float32).astype(jnp.bfloat16)
        rank = jnp.dot(as_bf16(mine), as_bf16(earlier), preferred_element_type=jnp.float32)
        code = code.astype(jnp.float32)
        lane = lax.broadcasted_iota(jnp.int32, (16, 128), 1)
        total = jnp.zeros((16, 128), jnp.float32)
        for k in range(CAP):
            found = jnp.sum(jnp.where(mine & (rank == k), code, 0.0), axis=1, keepdims=True)
            total = jnp.where(lane == k, found, total)
        listed[...] = total.astype(jnp.int32)
        copy = pltpu.make_async_copy(listed, table, table_sem)
        copy.start()
        copy.wait()
        for copy in copies:
            copy.wait()

    lane = lax.broadcasted_iota(jnp.int32, (TS, TS), 1)

    def tile(slot, carry):
        code = table[step * (CUT // CAP) + slot // CAP, slot % CAP]
        at = ((code >> 4) & 3) * 512 + ((code >> 6) & 255)
        dx = (code >> 14) & 255
        turn = (TS - dx) & (TS - 1)
        low = halves[pl.ds(at, TS), :]
        high = halves[pl.ds(at + 256, TS), :]
        mixed = jnp.where(lane >= dx, low, high).astype(jnp.bfloat16)
        send[slot] = pltpu.roll(mixed, turn, 1)
        return carry

    lax.fori_loop(0, CUT, tile, 0, unroll=CUT)


def weights_kernel(amp, moments, *outs):
    main, edge = outs[:6], outs[6]
    first_row = amp[0] * ROWS
    lane = lax.broadcasted_iota(jnp.int32, (SIDE, 128), 1)
    lane16 = lax.broadcasted_iota(jnp.int32, (EDGE, 128), 1)

    def across(rows, members, yh):
        total = jnp.broadcast_to(rows[members[0] : members[0] + 1], (yh.shape[0], 128))
        for power, member in enumerate(members[1:]):
            total = total + (yh if power == 0 else yh * yh) * rows[member : member + 1]
        return pltpu.roll(total, 0, 1, stride=1, stride_axis=0)

    for half in range(2):
        y = (first_row + half * SIDE + lax.broadcasted_iota(jnp.int32, (SIDE, 128), 0)).astype(jnp.float32)
        yh = (2.0 * y + 1.0) / 1024.0 - 1.0
        rim = slice(0, EDGE) if half == 0 else slice(SIDE - EDGE, SIDE)
        lead = 6 if half else -HALF
        rim_lead = EDGE - HALF if half == 0 else SIDE - EDGE + 6 - WIN
        for a, members in enumerate(((0, 2, 5), (1, 4), (3,))):
            held = jnp.zeros((SIDE, 128), jnp.float32)
            held_rim = jnp.zeros((EDGE, 128), jnp.float32)
            for u in range(TAPS):
                moment = moments[:, u * 128 : (u + 1) * 128]
                last = u == TAPS - 1
                group, low = u * WIN // 128, u * WIN % 128
                end = low + WIN
                turned = across(pltpu.roll(moment, (lead + low) % 128, 1), members, yh)
                held = jnp.where((lane >= low) & (lane < end), turned, held)
                if end >= 128 or last:
                    main[half * 3 + a][:, group * 128 : (group + 1) * 128] = held.astype(jnp.bfloat16)
                    held = jnp.where(lane < end - 128, turned, 0.0)
                    if last and end > 128:
                        main[half * 3 + a][:, (group + 1) * 128 : (group + 2) * 128] = held.astype(jnp.bfloat16)
                group, low = u * EDGE // 128, u * EDGE % 128
                turned = across(pltpu.roll(moment, (rim_lead + low) % 128, 1), members, yh[rim])
                held_rim = jnp.where((lane16 >= low) & (lane16 < low + EDGE), turned, held_rim)
                if low + EDGE == 128 or last:
                    at = slice(a * EDGE, (a + 1) * EDGE)
                    edge[half, at, group * 128 : (group + 1) * 128] = held_rim.astype(jnp.bfloat16)
                    held_rim = jnp.zeros((EDGE, 128), jnp.float32)
        edge[half, 3 * EDGE :, :] = pltpu.roll(edge[half, : 3 * EDGE, :], EDGE, 1)


def apart(transposed):
    wide, narrow = (1, 0) if transposed else (0, 1)
    column = lax.broadcasted_iota(jnp.int32, (256, 256), wide)
    place = lax.broadcasted_iota(jnp.int32, (256, 256), narrow)
    home = jnp.where(place < TS, 2 * place, 2 * place - 255)
    return (column == home).astype(jnp.float32).astype(jnp.bfloat16)


def phase_kernel(slots, tiles, far_weights, planes, top, bottom, near_weights, sem):
    copy = pltpu.make_async_copy(far_weights, near_weights, sem)
    copy.start()
    split = apart(False)
    for pair in range(16):
        both = jnp.concatenate([tiles[slots[2 * pair]], tiles[slots[2 * pair + 1]]], axis=1)
        moved = jnp.dot(both, split, preferred_element_type=jnp.float32).astype(jnp.bfloat16)
        for phase in range(2):
            piece = moved[:, phase * TS : (phase + 1) * TS]
            planes[phase, :, pair * TS : (pair + 1) * TS] = piece
            at = slice(phase * 2048 + pair * TS, phase * 2048 + (pair + 1) * TS)
            top[:, at] = piece[:EDGE]
            bottom[:, at] = piece[TS - EDGE :]
    copy.wait()


def fold(parts, first, rows):
    folded = []
    for phase, part in enumerate(parts):
        x = 2 * (first + lax.broadcasted_iota(jnp.int32, (rows, part.shape[1]), 1)) + phase
        xh = (2.0 * x.astype(jnp.float32) + 1.0) / 4096.0 - 1.0
        terms = [part[a * rows : (a + 1) * rows] for a in range(3)]
        folded.append(terms[0] + xh * (terms[1] + xh * terms[2]))
    return folded


def product(weights, lags):
    return [
        jnp.dot(
            weights,
            lags[phase : phase + TAPS].reshape(weights.shape[1], lags.shape[2]),
            preferred_element_type=jnp.float32,
        )
        for phase in range(2)
    ]


def together(pieces, join):
    rows = pieces[0].shape[0]
    both = jnp.concatenate(pieces, axis=0)
    high = both.astype(jnp.bfloat16)
    low = (both - high.astype(jnp.float32)).astype(jnp.bfloat16)
    moved = jnp.dot(jnp.concatenate([high, low], axis=0), join, preferred_element_type=jnp.float32)
    moved = moved[: both.shape[0]] + moved[both.shape[0] :]
    return [moved[i * rows : (i + 1) * rows] for i in range(len(pieces))]


def paired(folded, i):
    return jnp.concatenate([phase[:, i * TS : (i + 1) * TS] for phase in folded], axis=1)


def shifted_by(tiles, lag):
    if lag == 0:
        return tiles[1:-1]
    lane = lax.broadcasted_iota(jnp.int32, tiles[0].shape, 1)
    if lag > 0:
        mixed = [jnp.where(lane >= lag, tiles[i], tiles[i + 1]) for i in range(1, len(tiles) - 1)]
    else:
        mixed = [jnp.where(lane < TS + lag, tiles[i], tiles[i - 1]) for i in range(1, len(tiles) - 1)]
    return [pltpu.roll(tile, (-lag) % TS, 1) for tile in mixed]


def main_kernel(planes, *refs):
    weights, (science, out, even, odd) = refs[:6], refs[6:]
    step = pl.program_id(0)

    def shift(first, buffer):
        near = []
        for phase in range(2):
            tiles = [
                planes[phase, :, pl.ds(pl.multiple_of(jnp.clip(first + i, 0, 15) * TS, TS), TS)] for i in range(-1, TILES + 1)
            ]
            tiles[0] = jnp.where(first > 0, tiles[0], jnp.zeros_like(tiles[0]))
            tiles[-1] = jnp.where(first + TILES < 16, tiles[-1], jnp.zeros_like(tiles[-1]))
            near.append(tiles)
        for index in range(LAGS):
            lag = index - HALF
            for i, tile in enumerate(shifted_by(near[lag % 2], lag // 2)):
                buffer[index, :, i * TS : (i + 1) * TS] = tile

    def multiply(first, buffer):
        pieces = []
        for half in range(2):
            members = [weights[half * 3 + a][:, :K_MAIN] for a in range(3)]
            parts = product(jnp.concatenate(members, axis=0), buffer[:, half * 48 : half * 48 + WIN, :])
            folded = fold(parts, first * TS, SIDE)
            pieces += [paired(folded, i) for i in range(TILES)]
        return pieces

    @pl.when(step == 0)
    def _():
        shift(0, even)

    first = step * 2 * TILES
    shift(first + TILES, odd)
    pieces = multiply(first, even)
    shift(first + 2 * TILES, even)
    pieces += multiply(first + TILES, odd)
    for n, model in enumerate(together(pieces, apart(True))):
        block, half, i = n // (2 * TILES), n // TILES % 2, n % TILES
        at = slice(half * SIDE, (half + 1) * SIDE)
        columns = slice(block * BLOCK + i * 256, block * BLOCK + (i + 1) * 256)
        out[at, columns] = science[at, columns] - model


def rim_kernel(inner, above, below, weights, partial, out, shifted, ends, sems):
    zero = jnp.zeros((EDGE, TS), jnp.bfloat16)
    rows = [pl.ds(0, EDGE), pl.ds(ROWS - EDGE, EDGE)]
    for number in range(2):
        pltpu.make_async_copy(partial.at[rows[number]], ends.at[number], sems.at[0, number]).start()
    pieces = []
    for number, source in enumerate((above, below)):
        keep = inner[number] > 0
        near = []
        for phase in range(2):
            tiles = [source[:, phase * 2048 + i * TS : phase * 2048 + (i + 1) * TS] for i in range(16)]
            near.append([zero] + [jnp.where(keep, tile, zero) for tile in tiles] + [zero])
        for index in range(LAGS):
            lag = index - HALF
            for i, tile in enumerate(shifted_by(near[lag % 2], lag // 2)):
                shifted[number, index, :, i * TS : (i + 1) * TS] = tile
        for first in range(0, 16, 4):
            lags = shifted[number, :, :, first * TS : (first + 4) * TS].reshape(K_EDGE, 4 * TS)
            parts = jnp.dot(weights[number, :, :K_EDGE], lags, preferred_element_type=jnp.float32)
            parts = [parts[: 3 * EDGE], parts[3 * EDGE :]]
            folded = fold(parts, first * TS, EDGE)
            pieces += [paired(folded, i) for i in range(4)]
    models = together(pieces, apart(True))
    for number in range(2):
        pltpu.make_async_copy(partial.at[rows[number]], ends.at[number], sems.at[0, number]).wait()
        for i in range(16):
            at = slice(i * 256, (i + 1) * 256)
            ends[number, :, at] = ends[number, :, at] - models[number * 16 + i]
        pltpu.make_async_copy(ends.at[number], out.at[rows[number]], sems.at[1, number]).start()
    for number in range(2):
        pltpu.make_async_copy(ends.at[number], out.at[rows[number]], sems.at[1, number]).wait()


def per_device(science, patches, coeffs, tile_owner, tile_patch, tile_offset):
    ccd_id = lax.axis_index("ccd")
    amp_id = lax.axis_index("amp")
    here = jnp.stack([amp_id, ccd_id])

    far = lambda array: pltpu.with_memory_space_constraint(array, pltpu.HBM)
    whole = pl.BlockSpec(memory_space=pltpu.VMEM)
    scalars = pl.BlockSpec(memory_space=pltpu.SMEM)
    send = pl.pallas_call(
        cut_kernel,
        grid=(16 * CAP // CUT,),
        out_shape=pltpu.HBM((16 * CAP, TS, TS), jnp.bfloat16),
        in_specs=[scalars] + [pl.BlockSpec(memory_space=pl.ANY)] * 4,
        out_specs=pl.BlockSpec((CUT, TS, TS), lambda i: (i, 0, 0)),
        scratch_shapes=[
            pltpu.VMEM((4 * 2 * 256, TS), jnp.float32),
            pltpu.VMEM((16, 8, 32), jnp.int32),
            pltpu.VMEM((16, 8, 32), jnp.int32),
            pltpu.VMEM((16, 8, 2, 32), jnp.int32),
            pltpu.VMEM((16, 128), jnp.int32),
            pltpu.SMEM((16, 128), jnp.int32),
            pltpu.SemaphoreType.DMA((4, 2)),
            pltpu.SemaphoreType.DMA((3,)),
            pltpu.SemaphoreType.DMA,
        ],
        compiler_params=pltpu.CompilerParams(vmem_limit_bytes=10 * MIB),
        name="cut",
    )(
        here,
        far(tile_owner.reshape(16, 8, 32)),
        far(tile_patch),
        far(tile_offset.transpose(0, 1, 3, 2)),
        far(patches.reshape(4, 256, 256)),
    )
    tiles = lax.all_to_all(send.reshape(16, CAP * TS, TS), "ccd", 0, 0, tiled=True).reshape(16 * CAP, TS, TS)

    order = jnp.arange(32)
    mine = tile_owner[ccd_id, amp_id, :, 0]
    earlier = (mine[:, None] == mine[None, :]) & (order[None, :] < order[:, None])
    slots = mine * CAP + jnp.minimum(jnp.sum(earlier.astype(jnp.int32), axis=1), CAP - 1)

    moments = jnp.einsum("km,kl->ml", coeffs[0], jnp.asarray(basis_table()), precision=lax.Precision.HIGHEST)
    *main, edge = pl.pallas_call(
        weights_kernel,
        out_shape=(
            *([jax.ShapeDtypeStruct((SIDE, K_PAD), jnp.bfloat16)] * 5),
            pltpu.HBM((SIDE, K_PAD), jnp.bfloat16),
            jax.ShapeDtypeStruct((2, 6 * EDGE, K_EDGE_PAD), jnp.bfloat16),
        ),
        in_specs=[scalars, whole],
        out_specs=(whole,) * 7,
        compiler_params=pltpu.CompilerParams(vmem_limit_bytes=10 * MIB),
        cost_estimate=pl.CostEstimate(flops=50_000_000, bytes_accessed=2_000_000, transcendentals=0),
        name="weights",
    )(amp_id.reshape(1), moments)

    planes, top, bottom, main[5] = pl.pallas_call(
        phase_kernel,
        out_shape=(
            jax.ShapeDtypeStruct((2, ROWS, 2048), jnp.bfloat16),
            *([jax.ShapeDtypeStruct((EDGE, 4096), jnp.bfloat16)] * 2),
            jax.ShapeDtypeStruct((SIDE, K_PAD), jnp.bfloat16),
        ),
        in_specs=[scalars, whole, pl.BlockSpec(memory_space=pl.ANY)],
        out_specs=(whole,) * 4,
        scratch_shapes=[pltpu.SemaphoreType.DMA],
        compiler_params=pltpu.CompilerParams(vmem_limit_bytes=8 * MIB),
        name="phases",
    )(slots, tiles, far(main[5]))
    down = [(i, (i + 1) % 8) for i in range(8)]
    above = lax.ppermute(bottom, "amp", down)
    below = lax.ppermute(top, "amp", [(b, a) for a, b in down])

    columns = pl.BlockSpec((ROWS, 2 * BLOCK), lambda j: (0, j))
    partial = pl.pallas_call(
        main_kernel,
        grid=(4096 // (2 * BLOCK),),
        in_specs=[whole] * 7 + [columns],
        out_specs=columns,
        scratch_shapes=[pltpu.VMEM((LAGS, ROWS, WIDE), jnp.bfloat16)] * 2,
        out_shape=jax.ShapeDtypeStruct((ROWS, 4096), jnp.float32),
        compiler_params=pltpu.CompilerParams(vmem_limit_bytes=12 * MIB),
        cost_estimate=pl.CostEstimate(flops=11_000_000_000, bytes_accessed=8_000_000, transcendentals=0),
        name="main",
    )(planes, *main, science[0])

    inner = jnp.stack([amp_id > 0, amp_id < 7]).astype(jnp.int32)
    result = pl.pallas_call(
        rim_kernel,
        in_specs=[scalars, whole, whole, whole, pl.BlockSpec(memory_space=pl.ANY)],
        out_specs=pl.BlockSpec(memory_space=pl.ANY),
        scratch_shapes=[
            pltpu.VMEM((2, LAGS, EDGE, 2048), jnp.bfloat16),
            pltpu.VMEM((2, EDGE, 4096), jnp.float32),
            pltpu.SemaphoreType.DMA((2, 2)),
        ],
        out_shape=jax.ShapeDtypeStruct((ROWS, 4096), jnp.float32),
        input_output_aliases={4: 0},
        compiler_params=pltpu.CompilerParams(vmem_limit_bytes=10 * MIB),
        name="rim",
    )(inner, above, below, edge, partial)
    return result[None]


def solution(mesh):
    placed = (
        P("ccd", "amp", None),
        P("ccd", "amp", None, None, None),
        P("ccd", None, None),
        P(),
        P(),
        P(),
    )
    return jax.shard_map(
        per_device, mesh=mesh, in_specs=placed, out_specs=P("ccd", "amp", None), check_vma=False
    )
```

```python
import numpy as np

import jax
import jax.numpy as jnp
import ml_dtypes
from jax import lax
from jax.experimental import pallas as pl
from jax.experimental.pallas import tpu as pltpu
from jax.sharding import PartitionSpec as P

TS = 128
HALF = 10
TAPS = 2 * HALF + 1
CAP = 4
WIDTHS = (1.0, 2.0, 4.0)
DEGREES = (4, 4, 3)
ROWS = 128
SIDE = 64
WIN = 80
EDGE = 16
K_MAIN = TAPS * WIN
K_PAD = 1792
K_EDGE = (TAPS + 1) * EDGE
K_EDGE_PAD = 384
BLOCK = 512
WIDE = BLOCK // 2
TILES = WIDE // TS
LAGS = TAPS + 1
CUT = 32
MIB = 1 << 20


def factor_table():
    offsets = np.arange(-HALF, HALF + 1).astype(np.float64)
    shapes = []
    for width, degree in zip(WIDTHS, DEGREES):
        for power in range(degree + 1):
            profile = np.exp(-offsets * offsets / (2.0 * width * width)) * (offsets / HALF) ** power
            shapes.append(profile / np.sum(np.abs(profile)))
    return np.stack(shapes).astype(np.float32).astype(ml_dtypes.bfloat16).astype(np.float32)


def basis_table():
    factors = factor_table()
    rows = []
    first = 0
    for degree in DEGREES:
        for p in range(degree + 1):
            for q in range(degree + 1 - p):
                grid = np.zeros((TAPS, 128), np.float32)
                grid[:, :TAPS] = factors[first + p][:, None] * factors[first + q][None, :]
                rows.append(grid.reshape(-1))
        first += degree + 1
    return np.stack(rows)


def cut_kernel(here, owners, numbers, offsets, patches, send, halves, *scratch):
    near_owners, near_numbers, near_offsets, listed, table, sems, index_sems, table_sem = scratch
    step = pl.program_id(0)

    @pl.when(step == 0)
    def _():
        copies = [
            pltpu.make_async_copy(
                patches.at[patch, :, pl.ds(side * TS, TS)],
                halves.at[pl.ds((patch * 2 + side) * 256, 256), :],
                sems.at[patch, side],
            )
            for patch in range(4)
            for side in range(2)
        ]
        indices = [
            pltpu.make_async_copy(owners, near_owners, index_sems.at[0]),
            pltpu.make_async_copy(numbers, near_numbers, index_sems.at[1]),
            pltpu.make_async_copy(offsets, near_offsets, index_sems.at[2]),
        ]
        for copy in indices + copies:
            copy.start()
        for copy in indices:
            copy.wait()
        strips = lambda array: array[:, pl.ds(here[0], 1), :].reshape(16, 32)
        owner = strips(near_owners)
        shift = near_offsets[:, pl.ds(here[0], 1)].reshape(16, 2, 32)
        code = owner + strips(near_numbers) * 16 + shift[:, 0] * 64 + shift[:, 1] * 16384
        mine = owner == here[1]
        earlier = lax.broadcasted_iota(jnp.int32, (32, 32), 0) < lax.broadcasted_iota(jnp.int32, (32, 32), 1)
        as_bf16 = lambda mask: mask.astype(jnp.float32).astype(jnp.bfloat16)
        rank = jnp.dot(as_bf16(mine), as_bf16(earlier), preferred_element_type=jnp.float32)
        code = code.astype(jnp.float32)
        lane = lax.broadcasted_iota(jnp.int32, (16, 128), 1)
        total = jnp.zeros((16, 128), jnp.float32)
        for k in range(CAP):
            found = jnp.sum(jnp.where(mine & (rank == k), code, 0.0), axis=1, keepdims=True)
            total = jnp.where(lane == k, found, total)
        listed[...] = total.astype(jnp.int32)
        copy = pltpu.make_async_copy(listed, table, table_sem)
        copy.start()
        copy.wait()
        for copy in copies:
            copy.wait()

    lane = lax.broadcasted_iota(jnp.int32, (TS, TS), 1)

    def tile(slot, carry):
        code = table[step * (CUT // CAP) + slot // CAP, slot % CAP]
        at = ((code >> 4) & 3) * 512 + ((code >> 6) & 255)
        dx = (code >> 14) & 255
        turn = (TS - dx) & (TS - 1)
        low = halves[pl.ds(at, TS), :]
        high = halves[pl.ds(at + 256, TS), :]
        mixed = jnp.where(lane >= dx, low, high).astype(jnp.bfloat16)
        send[slot] = pltpu.roll(mixed, turn, 1)
        return carry

    lax.fori_loop(0, CUT, tile, 0, unroll=CUT)


def weights_kernel(amp, moments, *outs):
    main, edge = outs[:6], outs[6]
    first_row = amp[0] * ROWS
    lane = lax.broadcasted_iota(jnp.int32, (SIDE, 128), 1)
    lane16 = lax.broadcasted_iota(jnp.int32, (EDGE, 128), 1)

    def across(rows, members, yh):
        total = jnp.broadcast_to(rows[members[0] : members[0] + 1], (yh.shape[0], 128))
        for power, member in enumerate(members[1:]):
            total = total + (yh if power == 0 else yh * yh) * rows[member : member + 1]
        return pltpu.roll(total, 0, 1, stride=1, stride_axis=0)

    for half in range(2):
        y = (first_row + half * SIDE + lax.broadcasted_iota(jnp.int32, (SIDE, 128), 0)).astype(jnp.float32)
        yh = (2.0 * y + 1.0) / 1024.0 - 1.0
        rim = slice(0, EDGE) if half == 0 else slice(SIDE - EDGE, SIDE)
        lead = 6 if half else -HALF
        rim_lead = EDGE - HALF if half == 0 else SIDE - EDGE + 6 - WIN
        for a, members in enumerate(((0, 2, 5), (1, 4), (3,))):
            held = jnp.zeros((SIDE, 128), jnp.float32)
            held_rim = jnp.zeros((EDGE, 128), jnp.float32)
            for u in range(TAPS):
                moment = moments[:, u * 128 : (u + 1) * 128]
                last = u == TAPS - 1
                group, low = u * WIN // 128, u * WIN % 128
                end = low + WIN
                turned = across(pltpu.roll(moment, (lead + low) % 128, 1), members, yh)
                held = jnp.where((lane >= low) & (lane < end), turned, held)
                if end >= 128 or last:
                    main[half * 3 + a][:, group * 128 : (group + 1) * 128] = held.astype(jnp.bfloat16)
                    held = jnp.where(lane < end - 128, turned, 0.0)
                    if last and end > 128:
                        main[half * 3 + a][:, (group + 1) * 128 : (group + 2) * 128] = held.astype(jnp.bfloat16)
                group, low = u * EDGE // 128, u * EDGE % 128
                turned = across(pltpu.roll(moment, (rim_lead + low) % 128, 1), members, yh[rim])
                held_rim = jnp.where((lane16 >= low) & (lane16 < low + EDGE), turned, held_rim)
                if low + EDGE == 128 or last:
                    at = slice(a * EDGE, (a + 1) * EDGE)
                    edge[half, at, group * 128 : (group + 1) * 128] = held_rim.astype(jnp.bfloat16)
                    held_rim = jnp.zeros((EDGE, 128), jnp.float32)
        edge[half, 3 * EDGE :, :] = pltpu.roll(edge[half, : 3 * EDGE, :], EDGE, 1)


def apart(transposed):
    wide, narrow = (1, 0) if transposed else (0, 1)
    column = lax.broadcasted_iota(jnp.int32, (256, 256), wide)
    place = lax.broadcasted_iota(jnp.int32, (256, 256), narrow)
    home = jnp.where(place < TS, 2 * place, 2 * place - 255)
    return (column == home).astype(jnp.float32).astype(jnp.bfloat16)


def phase_kernel(slots, tiles, planes, top, bottom):
    split = apart(False)
    for pair in range(16):
        both = jnp.concatenate([tiles[slots[2 * pair]], tiles[slots[2 * pair + 1]]], axis=1)
        moved = jnp.dot(both, split, preferred_element_type=jnp.float32).astype(jnp.bfloat16)
        for phase in range(2):
            piece = moved[:, phase * TS : (phase + 1) * TS]
            planes[phase, :, pair * TS : (pair + 1) * TS] = piece
            at = slice(phase * 2048 + pair * TS, phase * 2048 + (pair + 1) * TS)
            top[:, at] = piece[:EDGE]
            bottom[:, at] = piece[TS - EDGE :]


def fold(parts, first, rows):
    folded = []
    for phase, part in enumerate(parts):
        x = 2 * (first + lax.broadcasted_iota(jnp.int32, (rows, part.shape[1]), 1)) + phase
        xh = (2.0 * x.astype(jnp.float32) + 1.0) / 4096.0 - 1.0
        terms = [part[a * rows : (a + 1) * rows] for a in range(3)]
        folded.append(terms[0] + xh * (terms[1] + xh * terms[2]))
    return folded


def product(weights, lags):
    return [
        jnp.dot(
            weights,
            lags[phase : phase + TAPS].reshape(weights.shape[1], lags.shape[2]),
            preferred_element_type=jnp.float32,
        )
        for phase in range(2)
    ]


def together(pieces, join):
    rows = pieces[0].shape[0]
    both = jnp.concatenate(pieces, axis=0)
    high = both.astype(jnp.bfloat16)
    low = (both - high.astype(jnp.float32)).astype(jnp.bfloat16)
    moved = jnp.dot(jnp.concatenate([high, low], axis=0), join, preferred_element_type=jnp.float32)
    moved = moved[: both.shape[0]] + moved[both.shape[0] :]
    return [moved[i * rows : (i + 1) * rows] for i in range(len(pieces))]


def paired(folded, i):
    return jnp.concatenate([phase[:, i * TS : (i + 1) * TS] for phase in folded], axis=1)


def shifted_by(tiles, lag):
    if lag == 0:
        return tiles[1:-1]
    lane = lax.broadcasted_iota(jnp.int32, tiles[0].shape, 1)
    if lag > 0:
        mixed = [jnp.where(lane >= lag, tiles[i], tiles[i + 1]) for i in range(1, len(tiles) - 1)]
    else:
        mixed = [jnp.where(lane < TS + lag, tiles[i], tiles[i - 1]) for i in range(1, len(tiles) - 1)]
    return [pltpu.roll(tile, (-lag) % TS, 1) for tile in mixed]


def main_kernel(planes, *refs):
    weights, (science, out, even, odd) = refs[:6], refs[6:]
    step = pl.program_id(0)

    def shift(first, buffer):
        near = []
        for phase in range(2):
            tiles = [
                planes[phase, :, pl.ds(pl.multiple_of(jnp.clip(first + i, 0, 15) * TS, TS), TS)] for i in range(-1, TILES + 1)
            ]
            tiles[0] = jnp.where(first > 0, tiles[0], jnp.zeros_like(tiles[0]))
            tiles[-1] = jnp.where(first + TILES < 16, tiles[-1], jnp.zeros_like(tiles[-1]))
            near.append(tiles)
        for index in range(LAGS):
            lag = index - HALF
            for i, tile in enumerate(shifted_by(near[lag % 2], lag // 2)):
                buffer[index, :, i * TS : (i + 1) * TS] = tile

    def multiply(first, buffer):
        pieces = []
        for half in range(2):
            members = [weights[half * 3 + a][:, :K_MAIN] for a in range(3)]
            parts = product(jnp.concatenate(members, axis=0), buffer[:, half * 48 : half * 48 + WIN, :])
            folded = fold(parts, first * TS, SIDE)
            pieces += [paired(folded, i) for i in range(TILES)]
        return pieces

    @pl.when(step == 0)
    def _():
        shift(0, even)

    first = step * 2 * TILES
    shift(first + TILES, odd)
    pieces = multiply(first, even)
    shift(first + 2 * TILES, even)
    pieces += multiply(first + TILES, odd)
    for n, model in enumerate(together(pieces, apart(True))):
        block, half, i = n // (2 * TILES), n // TILES % 2, n % TILES
        at = slice(half * SIDE, (half + 1) * SIDE)
        columns = slice(block * BLOCK + i * 256, block * BLOCK + (i + 1) * 256)
        out[at, columns] = science[at, columns] - model


def rim_kernel(inner, above, below, far_weights, partial, out, shifted, ends, weights, sems, weights_sem):
    copy = pltpu.make_async_copy(far_weights, weights, weights_sem)
    copy.start()
    zero = jnp.zeros((EDGE, TS), jnp.bfloat16)
    rows = [pl.ds(0, EDGE), pl.ds(ROWS - EDGE, EDGE)]
    for number in range(2):
        pltpu.make_async_copy(partial.at[rows[number]], ends.at[number], sems.at[0, number]).start()
    pieces = []
    for number, source in enumerate((above, below)):
        keep = inner[number] > 0
        near = []
        for phase in range(2):
            tiles = [source[:, phase * 2048 + i * TS : phase * 2048 + (i + 1) * TS] for i in range(16)]
            near.append([zero] + [jnp.where(keep, tile, zero) for tile in tiles] + [zero])
        for index in range(LAGS):
            lag = index - HALF
            for i, tile in enumerate(shifted_by(near[lag % 2], lag // 2)):
                shifted[number, index, :, i * TS : (i + 1) * TS] = tile
    copy.wait()
    for number in range(2):
        for first in range(0, 16, 4):
            lags = shifted[number, :, :, first * TS : (first + 4) * TS].reshape(K_EDGE, 4 * TS)
            parts = jnp.dot(weights[number, :, :K_EDGE], lags, preferred_element_type=jnp.float32)
            parts = [parts[: 3 * EDGE], parts[3 * EDGE :]]
            folded = fold(parts, first * TS, EDGE)
            pieces += [paired(folded, i) for i in range(4)]
    models = together(pieces, apart(True))
    for number in range(2):
        pltpu.make_async_copy(partial.at[rows[number]], ends.at[number], sems.at[0, number]).wait()
        for i in range(16):
            at = slice(i * 256, (i + 1) * 256)
            ends[number, :, at] = ends[number, :, at] - models[number * 16 + i]
        pltpu.make_async_copy(ends.at[number], out.at[rows[number]], sems.at[1, number]).start()
    for number in range(2):
        pltpu.make_async_copy(ends.at[number], out.at[rows[number]], sems.at[1, number]).wait()


def per_device(science, patches, coeffs, tile_owner, tile_patch, tile_offset):
    ccd_id = lax.axis_index("ccd")
    amp_id = lax.axis_index("amp")
    here = jnp.stack([amp_id, ccd_id])

    far = lambda array: pltpu.with_memory_space_constraint(array, pltpu.HBM)
    whole = pl.BlockSpec(memory_space=pltpu.VMEM)
    scalars = pl.BlockSpec(memory_space=pltpu.SMEM)
    send = pl.pallas_call(
        cut_kernel,
        grid=(16 * CAP // CUT,),
        out_shape=pltpu.HBM((16 * CAP, TS, TS), jnp.bfloat16),
        in_specs=[scalars] + [pl.BlockSpec(memory_space=pl.ANY)] * 4,
        out_specs=pl.BlockSpec((CUT, TS, TS), lambda i: (i, 0, 0)),
        scratch_shapes=[
            pltpu.VMEM((4 * 2 * 256, TS), jnp.float32),
            pltpu.VMEM((16, 8, 32), jnp.int32),
            pltpu.VMEM((16, 8, 32), jnp.int32),
            pltpu.VMEM((16, 8, 2, 32), jnp.int32),
            pltpu.VMEM((16, 128), jnp.int32),
            pltpu.SMEM((16, 128), jnp.int32),
            pltpu.SemaphoreType.DMA((4, 2)),
            pltpu.SemaphoreType.DMA((3,)),
            pltpu.SemaphoreType.DMA,
        ],
        compiler_params=pltpu.CompilerParams(vmem_limit_bytes=10 * MIB),
        name="cut",
    )(
        here,
        far(tile_owner.reshape(16, 8, 32)),
        far(tile_patch),
        far(tile_offset.transpose(0, 1, 3, 2)),
        far(patches.reshape(4, 256, 256)),
    )
    tiles = lax.all_to_all(send.reshape(16, CAP * TS, TS), "ccd", 0, 0, tiled=True).reshape(16 * CAP, TS, TS)

    order = jnp.arange(32)
    mine = tile_owner[ccd_id, amp_id, :, 0]
    earlier = (mine[:, None] == mine[None, :]) & (order[None, :] < order[:, None])
    slots = mine * CAP + jnp.minimum(jnp.sum(earlier.astype(jnp.int32), axis=1), CAP - 1)

    moments = jnp.einsum("km,kl->ml", coeffs[0], jnp.asarray(basis_table()), precision=lax.Precision.HIGHEST)
    *main, edge = pl.pallas_call(
        weights_kernel,
        out_shape=(
            *([jax.ShapeDtypeStruct((SIDE, K_PAD), jnp.bfloat16)] * 6),
            pltpu.HBM((2, 6 * EDGE, K_EDGE_PAD), jnp.bfloat16),
        ),
        in_specs=[scalars, whole],
        out_specs=(whole,) * 7,
        compiler_params=pltpu.CompilerParams(vmem_limit_bytes=10 * MIB),
        cost_estimate=pl.CostEstimate(flops=50_000_000, bytes_accessed=2_000_000, transcendentals=0),
        name="weights",
    )(amp_id.reshape(1), moments)

    planes, top, bottom = pl.pallas_call(
        phase_kernel,
        out_shape=(
            jax.ShapeDtypeStruct((2, ROWS, 2048), jnp.bfloat16),
            *([jax.ShapeDtypeStruct((EDGE, 4096), jnp.bfloat16)] * 2),
        ),
        in_specs=[scalars, whole],
        out_specs=(whole,) * 3,
        compiler_params=pltpu.CompilerParams(vmem_limit_bytes=8 * MIB),
        name="phases",
    )(slots, tiles)
    down = [(i, (i + 1) % 8) for i in range(8)]
    above = lax.ppermute(bottom, "amp", down)
    below = lax.ppermute(top, "amp", [(b, a) for a, b in down])

    columns = pl.BlockSpec((ROWS, 2 * BLOCK), lambda j: (0, j))
    partial = pl.pallas_call(
        main_kernel,
        grid=(4096 // (2 * BLOCK),),
        in_specs=[whole] * 7 + [columns],
        out_specs=columns,
        scratch_shapes=[pltpu.VMEM((LAGS, ROWS, WIDE), jnp.bfloat16)] * 2,
        out_shape=jax.ShapeDtypeStruct((ROWS, 4096), jnp.float32),
        compiler_params=pltpu.CompilerParams(vmem_limit_bytes=12 * MIB),
        cost_estimate=pl.CostEstimate(flops=11_000_000_000, bytes_accessed=8_000_000, transcendentals=0),
        name="main",
    )(planes, *main, science[0])

    inner = jnp.stack([amp_id > 0, amp_id < 7]).astype(jnp.int32)
    result = pl.pallas_call(
        rim_kernel,
        in_specs=[scalars, whole, whole] + [pl.BlockSpec(memory_space=pl.ANY)] * 2,
        out_specs=pl.BlockSpec(memory_space=pl.ANY),
        scratch_shapes=[
            pltpu.VMEM((2, LAGS, EDGE, 2048), jnp.bfloat16),
            pltpu.VMEM((2, EDGE, 4096), jnp.float32),
            pltpu.VMEM((2, 6 * EDGE, K_EDGE_PAD), jnp.bfloat16),
            pltpu.SemaphoreType.DMA((2, 2)),
            pltpu.SemaphoreType.DMA,
        ],
        out_shape=jax.ShapeDtypeStruct((ROWS, 4096), jnp.float32),
        input_output_aliases={4: 0},
        compiler_params=pltpu.CompilerParams(vmem_limit_bytes=10 * MIB),
        name="rim",
    )(inner, above, below, far(edge), partial)
    return result[None]


def solution(mesh):
    placed = (
        P("ccd", "amp", None),
        P("ccd", "amp", None, None, None),
        P("ccd", None, None),
        P(),
        P(),
        P(),
    )
    return jax.shard_map(
        per_device, mesh=mesh, in_specs=placed, out_specs=P("ccd", "amp", None), check_vma=False
    )
```

```python
import numpy as np

import jax
import jax.numpy as jnp
import ml_dtypes
from jax import lax
from jax.experimental import pallas as pl
from jax.experimental.pallas import tpu as pltpu
from jax.sharding import PartitionSpec as P

TS = 128
HALF = 10
TAPS = 2 * HALF + 1
CAP = 4
WIDTHS = (1.0, 2.0, 4.0)
DEGREES = (4, 4, 3)
ROWS = 128
SIDE = 64
WIN = 80
EDGE = 16
K_MAIN = TAPS * WIN
K_PAD = 1792
K_EDGE = (TAPS + 1) * EDGE
K_EDGE_PAD = 384
BLOCK = 512
WIDE = BLOCK // 2
TILES = WIDE // TS
LAGS = TAPS + 1
CUT = 32
MIB = 1 << 20


def factor_table():
    offsets = np.arange(-HALF, HALF + 1).astype(np.float64)
    shapes = []
    for width, degree in zip(WIDTHS, DEGREES):
        for power in range(degree + 1):
            profile = np.exp(-offsets * offsets / (2.0 * width * width)) * (offsets / HALF) ** power
            shapes.append(profile / np.sum(np.abs(profile)))
    return np.stack(shapes).astype(np.float32).astype(ml_dtypes.bfloat16).astype(np.float32)


def basis_table():
    factors = factor_table()
    rows = []
    first = 0
    for degree in DEGREES:
        for p in range(degree + 1):
            for q in range(degree + 1 - p):
                grid = np.zeros((TAPS, 128), np.float32)
                grid[:, :TAPS] = factors[first + p][:, None] * factors[first + q][None, :]
                rows.append(grid.reshape(-1))
        first += degree + 1
    return np.stack(rows)


def cut_kernel(here, owners, numbers, offsets, patches, send, halves, *scratch):
    near_owners, near_numbers, near_offsets, listed, table, sems, index_sems, table_sem = scratch
    step = pl.program_id(0)

    @pl.when(step == 0)
    def _():
        copies = [
            pltpu.make_async_copy(
                patches.at[patch, :, pl.ds(side * TS, TS)],
                halves.at[pl.ds((patch * 2 + side) * 256, 256), :],
                sems.at[patch, side],
            )
            for patch in range(4)
            for side in range(2)
        ]
        indices = [
            pltpu.make_async_copy(owners, near_owners, index_sems.at[0]),
            pltpu.make_async_copy(numbers, near_numbers, index_sems.at[1]),
            pltpu.make_async_copy(offsets, near_offsets, index_sems.at[2]),
        ]
        for copy in indices + copies:
            copy.start()
        for copy in indices:
            copy.wait()
        strips = lambda array: array[:, pl.ds(here[0], 1), :].reshape(16, 32)
        owner = strips(near_owners)
        shift = near_offsets[:, pl.ds(here[0], 1)].reshape(16, 2, 32)
        code = owner + strips(near_numbers) * 16 + shift[:, 0] * 64 + shift[:, 1] * 16384
        mine = owner == here[1]
        earlier = lax.broadcasted_iota(jnp.int32, (32, 32), 0) < lax.broadcasted_iota(jnp.int32, (32, 32), 1)
        as_bf16 = lambda mask: mask.astype(jnp.float32).astype(jnp.bfloat16)
        rank = jnp.dot(as_bf16(mine), as_bf16(earlier), preferred_element_type=jnp.float32)
        code = code.astype(jnp.float32)
        lane = lax.broadcasted_iota(jnp.int32, (16, 128), 1)
        total = jnp.zeros((16, 128), jnp.float32)
        for k in range(CAP):
            found = jnp.sum(jnp.where(mine & (rank == k), code, 0.0), axis=1, keepdims=True)
            total = jnp.where(lane == k, found, total)
        listed[...] = total.astype(jnp.int32)
        copy = pltpu.make_async_copy(listed, table, table_sem)
        copy.start()
        copy.wait()
        for copy in copies:
            copy.wait()

    lane = lax.broadcasted_iota(jnp.int32, (TS, TS), 1)

    def tile(slot, carry):
        code = table[step * (CUT // CAP) + slot // CAP, slot % CAP]
        at = ((code >> 4) & 3) * 512 + ((code >> 6) & 255)
        dx = (code >> 14) & 255
        turn = (TS - dx) & (TS - 1)
        low = halves[pl.ds(at, TS), :]
        high = halves[pl.ds(at + 256, TS), :]
        mixed = jnp.where(lane >= dx, low, high).astype(jnp.bfloat16)
        send[slot] = pltpu.roll(mixed, turn, 1)
        return carry

    lax.fori_loop(0, CUT, tile, 0, unroll=CUT)


def weights_kernel(amp, moments, *outs):
    main, edge = outs[:6], outs[6]
    first_row = amp[0] * ROWS
    lane = lax.broadcasted_iota(jnp.int32, (SIDE, 128), 1)
    lane16 = lax.broadcasted_iota(jnp.int32, (EDGE, 128), 1)

    def across(rows, members, yh):
        total = jnp.broadcast_to(rows[members[0] : members[0] + 1], (yh.shape[0], 128))
        for power, member in enumerate(members[1:]):
            total = total + (yh if power == 0 else yh * yh) * rows[member : member + 1]
        return pltpu.roll(total, 0, 1, stride=1, stride_axis=0)

    for half in range(2):
        y = (first_row + half * SIDE + lax.broadcasted_iota(jnp.int32, (SIDE, 128), 0)).astype(jnp.float32)
        yh = (2.0 * y + 1.0) / 1024.0 - 1.0
        rim = slice(0, EDGE) if half == 0 else slice(SIDE - EDGE, SIDE)
        lead = 6 if half else -HALF
        rim_lead = EDGE - HALF if half == 0 else SIDE - EDGE + 6 - WIN
        for a, members in enumerate(((0, 2, 5), (1, 4), (3,))):
            held = jnp.zeros((SIDE, 128), jnp.float32)
            held_rim = jnp.zeros((EDGE, 128), jnp.float32)
            for u in range(TAPS):
                moment = moments[:, u * 128 : (u + 1) * 128]
                last = u == TAPS - 1
                group, low = u * WIN // 128, u * WIN % 128
                end = low + WIN
                turned = across(pltpu.roll(moment, (lead + low) % 128, 1), members, yh)
                held = jnp.where((lane >= low) & (lane < end), turned, held)
                if end >= 128 or last:
                    main[half * 3 + a][:, group * 128 : (group + 1) * 128] = held.astype(jnp.bfloat16)
                    held = jnp.where(lane < end - 128, turned, 0.0)
                    if last and end > 128:
                        main[half * 3 + a][:, (group + 1) * 128 : (group + 2) * 128] = held.astype(jnp.bfloat16)
                group, low = u * EDGE // 128, u * EDGE % 128
                turned = across(pltpu.roll(moment, (rim_lead + low) % 128, 1), members, yh[rim])
                held_rim = jnp.where((lane16 >= low) & (lane16 < low + EDGE), turned, held_rim)
                if low + EDGE == 128 or last:
                    at = slice(a * EDGE, (a + 1) * EDGE)
                    edge[half, at, group * 128 : (group + 1) * 128] = held_rim.astype(jnp.bfloat16)
                    held_rim = jnp.zeros((EDGE, 128), jnp.float32)
        edge[half, 3 * EDGE :, :] = pltpu.roll(edge[half, : 3 * EDGE, :], EDGE, 1)


def apart(transposed):
    wide, narrow = (1, 0) if transposed else (0, 1)
    column = lax.broadcasted_iota(jnp.int32, (256, 256), wide)
    place = lax.broadcasted_iota(jnp.int32, (256, 256), narrow)
    home = jnp.where(place < TS, 2 * place, 2 * place - 255)
    return (column == home).astype(jnp.float32).astype(jnp.bfloat16)


def phase_kernel(slots, tiles, planes, top, bottom):
    split = apart(False)
    for pair in range(16):
        both = jnp.concatenate([tiles[slots[2 * pair]], tiles[slots[2 * pair + 1]]], axis=1)
        moved = jnp.dot(both, split, preferred_element_type=jnp.float32).astype(jnp.bfloat16)
        for phase in range(2):
            piece = moved[:, phase * TS : (phase + 1) * TS]
            planes[phase, :, pair * TS : (pair + 1) * TS] = piece
            at = slice(phase * 2048 + pair * TS, phase * 2048 + (pair + 1) * TS)
            top[:, at] = piece[:EDGE]
            bottom[:, at] = piece[TS - EDGE :]


def fold(parts, first, rows):
    folded = []
    for phase, part in enumerate(parts):
        x = 2 * (first + lax.broadcasted_iota(jnp.int32, (rows, part.shape[1]), 1)) + phase
        xh = (2.0 * x.astype(jnp.float32) + 1.0) / 4096.0 - 1.0
        terms = [part[a * rows : (a + 1) * rows] for a in range(3)]
        folded.append(terms[0] + xh * (terms[1] + xh * terms[2]))
    return folded


def product(weights, lags):
    return [
        jnp.dot(
            weights,
            lags[phase : phase + TAPS].reshape(weights.shape[1], lags.shape[2]),
            preferred_element_type=jnp.float32,
        )
        for phase in range(2)
    ]


def together(pieces, join):
    rows = pieces[0].shape[0]
    both = jnp.concatenate(pieces, axis=0)
    high = both.astype(jnp.bfloat16)
    low = (both - high.astype(jnp.float32)).astype(jnp.bfloat16)
    moved = jnp.dot(jnp.concatenate([high, low], axis=0), join, preferred_element_type=jnp.float32)
    moved = moved[: both.shape[0]] + moved[both.shape[0] :]
    return [moved[i * rows : (i + 1) * rows] for i in range(len(pieces))]


def paired(folded, i):
    return jnp.concatenate([phase[:, i * TS : (i + 1) * TS] for phase in folded], axis=1)


def shifted_by(tiles, lag):
    if lag == 0:
        return tiles[1:-1]
    lane = lax.broadcasted_iota(jnp.int32, tiles[0].shape, 1)
    if lag > 0:
        mixed = [jnp.where(lane >= lag, tiles[i], tiles[i + 1]) for i in range(1, len(tiles) - 1)]
    else:
        mixed = [jnp.where(lane < TS + lag, tiles[i], tiles[i - 1]) for i in range(1, len(tiles) - 1)]
    return [pltpu.roll(tile, (-lag) % TS, 1) for tile in mixed]


def main_kernel(planes, *refs):
    far_weights, (science, out, even, odd, held, sem) = refs[5], refs[6:]
    weights = (*refs[:5], held)
    step = pl.program_id(0)

    def shift(first, buffer):
        near = []
        for phase in range(2):
            tiles = [
                planes[phase, :, pl.ds(pl.multiple_of(jnp.clip(first + i, 0, 15) * TS, TS), TS)] for i in range(-1, TILES + 1)
            ]
            tiles[0] = jnp.where(first > 0, tiles[0], jnp.zeros_like(tiles[0]))
            tiles[-1] = jnp.where(first + TILES < 16, tiles[-1], jnp.zeros_like(tiles[-1]))
            near.append(tiles)
        for index in range(LAGS):
            lag = index - HALF
            for i, tile in enumerate(shifted_by(near[lag % 2], lag // 2)):
                buffer[index, :, i * TS : (i + 1) * TS] = tile

    def multiply(first, buffer):
        pieces = []
        for half in range(2):
            members = [weights[half * 3 + a][:, :K_MAIN] for a in range(3)]
            parts = product(jnp.concatenate(members, axis=0), buffer[:, half * 48 : half * 48 + WIN, :])
            folded = fold(parts, first * TS, SIDE)
            pieces += [paired(folded, i) for i in range(TILES)]
        return pieces

    @pl.when(step == 0)
    def _():
        copy = pltpu.make_async_copy(far_weights, held, sem)
        copy.start()
        shift(0, even)
        copy.wait()

    first = step * 2 * TILES
    shift(first + TILES, odd)
    pieces = multiply(first, even)
    shift(first + 2 * TILES, even)
    pieces += multiply(first + TILES, odd)
    for n, model in enumerate(together(pieces, apart(True))):
        block, half, i = n // (2 * TILES), n // TILES % 2, n % TILES
        at = slice(half * SIDE, (half + 1) * SIDE)
        columns = slice(block * BLOCK + i * 256, block * BLOCK + (i + 1) * 256)
        out[at, columns] = science[at, columns] - model


def rim_kernel(inner, above, below, weights, partial, out, shifted, ends, sems):
    zero = jnp.zeros((EDGE, TS), jnp.bfloat16)
    rows = [pl.ds(0, EDGE), pl.ds(ROWS - EDGE, EDGE)]
    for number in range(2):
        pltpu.make_async_copy(partial.at[rows[number]], ends.at[number], sems.at[0, number]).start()
    pieces = []
    for number, source in enumerate((above, below)):
        keep = inner[number] > 0
        near = []
        for phase in range(2):
            tiles = [source[:, phase * 2048 + i * TS : phase * 2048 + (i + 1) * TS] for i in range(16)]
            near.append([zero] + [jnp.where(keep, tile, zero) for tile in tiles] + [zero])
        for index in range(LAGS):
            lag = index - HALF
            for i, tile in enumerate(shifted_by(near[lag % 2], lag // 2)):
                shifted[number, index, :, i * TS : (i + 1) * TS] = tile
        for first in range(0, 16, 4):
            lags = shifted[number, :, :, first * TS : (first + 4) * TS].reshape(K_EDGE, 4 * TS)
            parts = jnp.dot(weights[number, :, :K_EDGE], lags, preferred_element_type=jnp.float32)
            parts = [parts[: 3 * EDGE], parts[3 * EDGE :]]
            folded = fold(parts, first * TS, EDGE)
            pieces += [paired(folded, i) for i in range(4)]
    models = together(pieces, apart(True))
    for number in range(2):
        pltpu.make_async_copy(partial.at[rows[number]], ends.at[number], sems.at[0, number]).wait()
        for i in range(16):
            at = slice(i * 256, (i + 1) * 256)
            ends[number, :, at] = ends[number, :, at] - models[number * 16 + i]
        pltpu.make_async_copy(ends.at[number], out.at[rows[number]], sems.at[1, number]).start()
    for number in range(2):
        pltpu.make_async_copy(ends.at[number], out.at[rows[number]], sems.at[1, number]).wait()


def per_device(science, patches, coeffs, tile_owner, tile_patch, tile_offset):
    ccd_id = lax.axis_index("ccd")
    amp_id = lax.axis_index("amp")
    here = jnp.stack([amp_id, ccd_id])

    far = lambda array: pltpu.with_memory_space_constraint(array, pltpu.HBM)
    whole = pl.BlockSpec(memory_space=pltpu.VMEM)
    scalars = pl.BlockSpec(memory_space=pltpu.SMEM)
    send = pl.pallas_call(
        cut_kernel,
        grid=(16 * CAP // CUT,),
        out_shape=pltpu.HBM((16 * CAP, TS, TS), jnp.bfloat16),
        in_specs=[scalars] + [pl.BlockSpec(memory_space=pl.ANY)] * 4,
        out_specs=pl.BlockSpec((CUT, TS, TS), lambda i: (i, 0, 0)),
        scratch_shapes=[
            pltpu.VMEM((4 * 2 * 256, TS), jnp.float32),
            pltpu.VMEM((16, 8, 32), jnp.int32),
            pltpu.VMEM((16, 8, 32), jnp.int32),
            pltpu.VMEM((16, 8, 2, 32), jnp.int32),
            pltpu.VMEM((16, 128), jnp.int32),
            pltpu.SMEM((16, 128), jnp.int32),
            pltpu.SemaphoreType.DMA((4, 2)),
            pltpu.SemaphoreType.DMA((3,)),
            pltpu.SemaphoreType.DMA,
        ],
        compiler_params=pltpu.CompilerParams(vmem_limit_bytes=10 * MIB),
        name="cut",
    )(
        here,
        far(tile_owner.reshape(16, 8, 32)),
        far(tile_patch),
        far(tile_offset.transpose(0, 1, 3, 2)),
        far(patches.reshape(4, 256, 256)),
    )
    tiles = lax.all_to_all(send.reshape(16, CAP * TS, TS), "ccd", 0, 0, tiled=True).reshape(16 * CAP, TS, TS)

    order = jnp.arange(32)
    mine = tile_owner[ccd_id, amp_id, :, 0]
    earlier = (mine[:, None] == mine[None, :]) & (order[None, :] < order[:, None])
    slots = mine * CAP + jnp.minimum(jnp.sum(earlier.astype(jnp.int32), axis=1), CAP - 1)

    moments = jnp.einsum("km,kl->ml", coeffs[0], jnp.asarray(basis_table()), precision=lax.Precision.HIGHEST)
    *main, edge = pl.pallas_call(
        weights_kernel,
        out_shape=(
            *([jax.ShapeDtypeStruct((SIDE, K_PAD), jnp.bfloat16)] * 5),
            pltpu.HBM((SIDE, K_PAD), jnp.bfloat16),
            jax.ShapeDtypeStruct((2, 6 * EDGE, K_EDGE_PAD), jnp.bfloat16),
        ),
        in_specs=[scalars, whole],
        out_specs=(whole,) * 7,
        compiler_params=pltpu.CompilerParams(vmem_limit_bytes=10 * MIB),
        cost_estimate=pl.CostEstimate(flops=50_000_000, bytes_accessed=2_000_000, transcendentals=0),
        name="weights",
    )(amp_id.reshape(1), moments)

    planes, top, bottom = pl.pallas_call(
        phase_kernel,
        out_shape=(
            jax.ShapeDtypeStruct((2, ROWS, 2048), jnp.bfloat16),
            *([jax.ShapeDtypeStruct((EDGE, 4096), jnp.bfloat16)] * 2),
        ),
        in_specs=[scalars, whole],
        out_specs=(whole,) * 3,
        compiler_params=pltpu.CompilerParams(vmem_limit_bytes=8 * MIB),
        name="phases",
    )(slots, tiles)
    down = [(i, (i + 1) % 8) for i in range(8)]
    above = lax.ppermute(bottom, "amp", down)
    below = lax.ppermute(top, "amp", [(b, a) for a, b in down])

    columns = pl.BlockSpec((ROWS, 2 * BLOCK), lambda j: (0, j))
    partial = pl.pallas_call(
        main_kernel,
        grid=(4096 // (2 * BLOCK),),
        in_specs=[whole] * 6 + [pl.BlockSpec(memory_space=pl.ANY), columns],
        out_specs=columns,
        scratch_shapes=[pltpu.VMEM((LAGS, ROWS, WIDE), jnp.bfloat16)] * 2
        + [pltpu.VMEM((SIDE, K_PAD), jnp.bfloat16), pltpu.SemaphoreType.DMA],
        out_shape=jax.ShapeDtypeStruct((ROWS, 4096), jnp.float32),
        compiler_params=pltpu.CompilerParams(vmem_limit_bytes=12 * MIB),
        cost_estimate=pl.CostEstimate(flops=11_000_000_000, bytes_accessed=8_000_000, transcendentals=0),
        name="main",
    )(planes, *main[:5], far(main[5]), science[0])

    inner = jnp.stack([amp_id > 0, amp_id < 7]).astype(jnp.int32)
    result = pl.pallas_call(
        rim_kernel,
        in_specs=[scalars, whole, whole, whole, pl.BlockSpec(memory_space=pl.ANY)],
        out_specs=pl.BlockSpec(memory_space=pl.ANY),
        scratch_shapes=[
            pltpu.VMEM((2, LAGS, EDGE, 2048), jnp.bfloat16),
            pltpu.VMEM((2, EDGE, 4096), jnp.float32),
            pltpu.SemaphoreType.DMA((2, 2)),
        ],
        out_shape=jax.ShapeDtypeStruct((ROWS, 4096), jnp.float32),
        input_output_aliases={4: 0},
        compiler_params=pltpu.CompilerParams(vmem_limit_bytes=10 * MIB),
        name="rim",
    )(inner, above, below, edge, partial)
    return result[None]


def solution(mesh):
    placed = (
        P("ccd", "amp", None),
        P("ccd", "amp", None, None, None),
        P("ccd", None, None),
        P(),
        P(),
        P(),
    )
    return jax.shard_map(
        per_device, mesh=mesh, in_specs=placed, out_specs=P("ccd", "amp", None), check_vma=False
    )
```
